256 devices in a mesh: tm: 128 (over y, z, x_lo, core), band: 2 (over x_hi).
Axes of the slice: x: 4 (x_hi: 2, x_lo: 2; x = x_hi * 2 + x_lo), y: 4, z: 8, core: 2. Of those that a mesh axis runs over, the one named last changes fastest.
Arguments:
- phonon: float32 [256, 256, 256], P('tm', 'band'), may hold values from -4 to 4
- momentum: float32 [256, 256, 256], P('tm', 'band'), may hold values from -6 to 6
- source: float32 [256, 256, 256], P('tm', 'band'), may hold values from -6 to 6
- guess: float32 [256, 256, 256], P('tm', 'band'), may hold values from -4 to 4
- bonds: int32 [2, 256, 256], P(None, 'band'), may hold values 0 or 1
Outputs:
- solution: float32 [256, 256, 256], P('tm', 'band')
- momentum_new: float32 [256, 256, 256], P('tm', 'band')
The draws below stay inside these ranges and needn't reach their ends.
All inputs are finite; a program needn't handle non-finite values. No bound on the sum of `bonds` on one device may be relied on, other than what follows from the above.
Results may differ from the reference program's by a relative error of at most 0.000064.
Values sent between devices are 32-bit elements; how exact they have to be, the bound alone decides.
A program may use at most 64 MiB of HBM per device.

```python
import math
import jax
import jax.numpy as jnp
from jax import lax

SLICES = 256
ROWS = 256
COLS = 256
ORDER = 24


def touch_ends(result, own_key, smallest, largest):
    longest = result.shape.index(max(result.shape))
    spots = []
    for shift in (0, 1):
        where = [jax.random.randint(jax.random.fold_in(own_key, axis), (), 0, length) for axis, length in enumerate(result.shape)]
        where[longest] = (where[longest] + shift) % result.shape[longest]
        spots.append(tuple(where))
    return result.at[spots[0]].set(smallest).at[spots[1]].set(largest)


def block_levels(own_key, extent, shards, least, largest):
    gain, own = 1.0, jax.random.fold_in(own_key, 6)
    for dim, blocks in shards:
        steps = jnp.exp(jax.random.uniform(jax.random.fold_in(own, dim), (blocks,), jnp.float32, least / len(shards), largest / len(shards)))
        gain = gain * jnp.repeat(steps, extent[dim] // blocks).reshape([-1 if axis == dim else 1 for axis in range(len(extent))])
    return gain


def noise(rng, dims, spread, bound, pieces=(), held_as=jnp.bfloat16):
    level = block_levels(rng, dims, pieces, -0.22, 0.18) if pieces else 1.0
    values = jax.random.normal(rng, dims, jnp.float32) * spread * level
    return jnp.minimum(jnp.maximum(values, -bound), bound).astype(held_as)


def setup_inputs(seed: int = 0) -> dict:
    key_list = jax.random.split(jax.random.key(seed), 6)
    phonon = noise(key_list[0], (SLICES, ROWS, COLS), 1.0, 4.0, ((0, 128), (1, 2)), jnp.float32)
    momentum = noise(key_list[1], (SLICES, ROWS, COLS), 1.0, 6.0, ((0, 128), (1, 2)), jnp.float32)
    source = noise(key_list[2], (SLICES, ROWS, COLS), 1.0, 6.0, ((0, 128), (1, 2)), jnp.float32)
    guess = noise(key_list[3], (SLICES, ROWS, COLS), 0.5, 4.0, ((0, 128), (1, 2)), jnp.float32)
    bonds = touch_ends((jax.random.randint(key_list[4], (2, ROWS, COLS), 0, 8) < 7).astype(jnp.int32), jax.random.fold_in(key_list[4], 1), 0, 1)
    return {"phonon": phonon, "momentum": momentum, "source": source, "guess": guess, "bonds": bonds}


hop_angle = 0.3
coupling = 0.2
stiffness = 1.0
mass_term = 0.5
relaxation = 0.25
step_size = 0.25
cheb_base = 4.03
cheb_slope = 0.5
half_width = 4.0

def dft_basis(length_total):
    rows = lax.broadcasted_iota(jnp.int32, (length_total, length_total), 0)
    columns = lax.broadcasted_iota(jnp.int32, (length_total, length_total), 1)
    phase = (2 * (rows // 2) + 1) * columns % (2 * length_total)
    angle = phase.astype(jnp.float32) * (math.pi / length_total)
    return math.sqrt(2.0 / length_total) * jnp.where(rows % 2 == 0, jnp.cos(angle), jnp.sin(angle))

def cheb_centre(index, length_total):
    angle = (2 * (index // 2) + 1).astype(jnp.float32) * (math.pi / length_total)
    return cheb_base + cheb_slope * (1.0 - jnp.cos(angle))

def pair_tables(horizontal, vertical, vertical_prev):
    grid_shape = horizontal.shape
    row_even = lax.broadcasted_iota(jnp.int32, grid_shape, 0) % 2 == 0
    column_even = lax.broadcasted_iota(jnp.int32, grid_shape, 1) % 2 == 0
    horizontal_prev = jnp.roll(horizontal, 1, 1)
    vertical_up = jnp.roll(vertical, 1, 0)
    strengths = (jnp.where(column_even, horizontal, horizontal_prev), jnp.where(column_even, horizontal_prev, horizontal), jnp.where(row_even, vertical, vertical_up), jnp.where(row_even, vertical_prev, vertical))
    return tuple(((jnp.cosh(hop_angle * strength), jnp.sinh(hop_angle * strength)) for strength in strengths))

def partner_of(vector, colour, row_even, column_even):
    if colour == 0:
        return jnp.where(column_even, jnp.roll(vector, -1, 2), jnp.roll(vector, 1, 2))
    if colour == 1:
        return jnp.where(column_even, jnp.roll(vector, 1, 2), jnp.roll(vector, -1, 2))
    if colour == 2:
        return jnp.where(row_even, jnp.roll(vector, -1, 1), jnp.roll(vector, 1, 1))
    return jnp.where(row_even, jnp.roll(vector, 1, 1), jnp.roll(vector, -1, 1))

def reference(phonon, momentum, source, guess, bonds):
    grid_shape = (ROWS, COLS)
    row_even = lax.broadcasted_iota(jnp.int32, grid_shape, 0) % 2 == 0
    column_even = lax.broadcasted_iota(jnp.int32, grid_shape, 1) % 2 == 0
    horizontal = bonds[0].astype(jnp.float32)
    vertical = bonds[1].astype(jnp.float32)
    tables = pair_tables(horizontal, vertical, jnp.roll(vertical, 1, 0))

    def apply_pairs(vector, colours):
        for colour in colours:
            cosh_part, sinh_part = tables[colour]
            vector = cosh_part * vector + sinh_part * partner_of(vector, colour, row_even, column_even)
        return vector
    expo = jnp.exp(-coupling * phonon)

    def apply_fwd(vector):
        return apply_pairs(expo * vector, (0, 1, 2, 3))
    applied = apply_fwd(guess)
    link = guess - jnp.concatenate([-applied[-1:], applied[:-1]], 0)
    shifted = jnp.concatenate([link[1:], -link[:1]], 0)
    normal = link - expo * apply_pairs(shifted, (3, 2, 1, 0))
    residual = source - normal
    basis = dft_basis(SLICES)
    spectrum = jnp.einsum('kl,lrc->krc', basis, residual, precision=lax.Precision.HIGHEST)
    centre = cheb_centre(jnp.arange(SLICES, dtype=jnp.int32), SLICES)[:, None, None]
    ratio = centre / half_width
    accum = jnp.zeros_like(spectrum)
    remaining = spectrum
    direction = spectrum / centre
    weight_now = 1.0 / ratio
    for counter in range(ORDER):
        beside_all = jnp.roll(direction, 1, 1) + jnp.roll(direction, -1, 1) + jnp.roll(direction, 1, 2) + jnp.roll(direction, -1, 2)
        accum = accum + direction
        remaining = remaining - (centre * direction - beside_all)
        weight_new = 1.0 / (2.0 * ratio - weight_now)
        direction = weight_new * weight_now * direction + 2.0 * weight_new / half_width * remaining
        weight_now = weight_new
    timed = jnp.einsum('kl,krc->lrc', basis, accum, precision=lax.Precision.HIGHEST)
    solution = guess + relaxation * timed
    propagated = apply_fwd(solution)
    image = solution - jnp.concatenate([-propagated[-1:], propagated[:-1]], 0)
    pulled = apply_pairs(jnp.concatenate([image[1:], -image[:1]], 0), (3, 2, 1, 0))
    fermion_force = -2.0 * coupling * expo * solution * pulled
    boson_force = stiffness * (2.0 * phonon - jnp.roll(phonon, 1, 0) - jnp.roll(phonon, -1, 0)) + mass_term * phonon
    momentum_new = momentum - step_size * (boson_force + fermion_force)
    return (solution, momentum_new)
```

```python
import functools
import math

import jax
import jax.numpy as jnp
import numpy as np
from jax import lax
from jax.experimental import pallas as pl
from jax.experimental.pallas import tpu as pltpu
from jax.sharding import PartitionSpec as P

ORDER = 24
hop_angle = 0.3
coupling = 0.2
stiffness = 1.0
mass_term = 0.5
relaxation = 0.25
step_size = 0.25
cheb_base = 4.03
cheb_slope = 0.5
half_width = 4.0

MESH = pl.DeviceIdType.MESH
HIGHEST = lax.Precision.HIGHEST
PAD = 8
COSH = math.cosh(hop_angle)
SINH = math.sinh(hop_angle)


def time_basis(length):
    k = np.arange(length)[:, None]
    l = np.arange(length)[None, :]
    angle = ((2 * (k // 2) + 1) * l % (2 * length)) * (math.pi / length)
    return (math.sqrt(2.0 / length) * np.where(k % 2 == 0, np.cos(angle), np.sin(angle))).astype(np.float32)


def space_basis(length):
    k = np.arange(length)
    m = (k + 1) // 2
    angle = (m[:, None] * np.arange(length)[None, :] % length) * (2.0 * math.pi / length)
    basis = np.where((k % 2 == 1)[:, None], np.cos(angle), np.sin(angle)) * math.sqrt(2.0 / length)
    basis[0] = 1.0 / math.sqrt(length)
    basis[-1] = np.where(np.arange(length) % 2 == 0, 1.0, -1.0) / math.sqrt(length)
    return basis.astype(np.float32), (2.0 * np.cos(2.0 * math.pi * m / length))


def cheb_tables(length):
    m = np.arange(length) // 2
    centre = cheb_base + cheb_slope * (1.0 - np.cos((2 * m + 1) * math.pi / length))
    ratio = centre / half_width
    rows = [centre, 1.0 / centre]
    weight = 1.0 / ratio
    for _ in range(ORDER - 1):
        new = 1.0 / (2.0 * ratio - weight)
        rows += [new * weight, 2.0 * new / half_width]
        weight = new
    while len(rows) % 8:
        rows.append(np.zeros(length))
    return np.stack(rows).astype(np.float32)


def wrap(value, size):
    return jnp.where(value >= size, value - size, value)


def kernel(
    steps, phonon, momentum, source, guess, bonds, tbasis, sbasis, weights, lams, lamv, sol_out, mom_out,
    ext, bond_ext, tables, expo, poly, y, r, v, w, sol, ssem, rsem, hs, hr, own_sem,
):
    n, lat = steps, phonon.shape[2]
    rows = phonon.shape[1]
    total = rows + 2 * PAD
    tm, band = lax.axis_index("tm"), lax.axis_index("band")
    other = 1 - band
    me = 2 * tm + band
    after = wrap(tm + 1, n)
    before = jnp.where(tm == 0, n - 1, tm - 1)

    barrier = pltpu.get_barrier_semaphore()
    pl.semaphore_signal(barrier, inc=1, device_id=(tm, other), device_id_type=MESH)

    def greet(i, carry):
        t = wrap(tm + i, n)
        pl.semaphore_signal(barrier, inc=1, device_id=(t, band), device_id_type=MESH)
        pl.semaphore_signal(barrier, inc=1, device_id=(t, other), device_id_type=MESH)
        return carry

    lax.fori_loop(1, n, greet, 0)
    own = pl.ds(PAD, rows)
    for s in range(2):
        ext[0, 1 + s, own, :] = phonon[s]
        ext[1, 1 + s, own, :] = guess[s]
        bond_ext[s, own, :] = bonds[s]
    pl.semaphore_wait(barrier, 2 * n - 1)

    low, high = pl.ds(PAD - 2, 2), pl.ds(PAD + rows, 2)
    first, last = pl.ds(PAD, 2), pl.ds(PAD + rows - 2, 2)

    def send(j, src, dst, device):
        copy = pltpu.make_async_remote_copy(
            src_ref=src, dst_ref=dst, send_sem=hs.at[j], recv_sem=hr.at[j], device_id=device, device_id_type=MESH
        )
        copy.start()
        return copy

    both = pl.ds(0, 2)
    halo = [
        send(0, ext.at[both, 2, own], ext.at[both, 0, own], (after, band)),
        send(1, ext.at[1, 1, own], ext.at[1, 3, own], (before, band)),
        send(2, ext.at[both, pl.ds(1, 2), last], ext.at[both, pl.ds(1, 2), low], (tm, other)),
        send(3, ext.at[both, pl.ds(1, 2), first], ext.at[both, pl.ds(1, 2), high], (tm, other)),
        send(4, bond_ext.at[both, last], bond_ext.at[both, low], (tm, other)),
        send(5, bond_ext.at[both, first], bond_ext.at[both, high], (tm, other)),
        send(6, ext.at[both, 2, last], ext.at[both, 0, low], (after, other)),
        send(7, ext.at[both, 2, first], ext.at[both, 0, high], (after, other)),
        send(8, ext.at[1, 1, last], ext.at[1, 3, low], (before, other)),
        send(9, ext.at[1, 1, first], ext.at[1, 3, high], (before, other)),
        send(10, ext.at[0, 1, own], ext.at[0, 3, own], (before, band)),
    ]
    for copy in halo[:10]:
        copy.wait_recv()

    row_even = lax.broadcasted_iota(jnp.int32, (total, lat), 0) % 2 == 0
    col_even = lax.broadcasted_iota(jnp.int32, (total, lat), 1) % 2 == 0

    def rolled(value, by, axis):
        return pltpu.roll(value, by % value.shape[axis], axis)

    horizontal, vertical = bond_ext[0], bond_ext[1]
    left, up = rolled(horizontal, 1, 1), rolled(vertical, 1, 0)
    strengths = (
        jnp.where(col_even, horizontal, left),
        jnp.where(col_even, left, horizontal),
        jnp.where(row_even, vertical, up),
        jnp.where(row_even, up, vertical),
    )
    for q, s in enumerate(strengths):
        tables[2 * q] = jnp.where(s == 1, COSH, 1.0).astype(jnp.float32)
        tables[2 * q + 1] = jnp.where(s == 1, SINH, 0.0).astype(jnp.float32)

    def pairs(value, colours):
        for q in colours:
            axis, even = (1, col_even) if q < 2 else (0, row_even)
            plus, minus = rolled(value, -1, axis), rolled(value, 1, axis)
            partner = jnp.where(even, plus, minus) if q % 2 == 0 else jnp.where(even, minus, plus)
            value = tables[2 * q] * value + tables[2 * q + 1] * partner
        return value

    ahead = (0, 1, 2, 3)
    back = (3, 2, 1, 0)
    sign_before = jnp.where(tm == 0, -1.0, 1.0).astype(jnp.float32)
    sign_after = jnp.where(tm == n - 1, -1.0, 1.0).astype(jnp.float32)

    for s in range(3):
        expo[s] = jnp.exp(-coupling * ext[0, s])

    inner = slice(PAD, PAD + rows)
    link_own = guess[0] - pairs(expo[0] * (sign_before * ext[1, 0]), ahead)[inner]
    for s in range(2):
        applied = pairs(expo[1 + s] * ext[1, 1 + s], ahead)
        link = (ext[1, 2] if s == 0 else sign_after * ext[1, 3]) - applied
        pulled = pairs(link, back)[inner]
        residual = source[s] - (link_own - expo[1 + s, own, :] * pulled)
        link_own = link[inner]
        turned = lax.dot_general(
            sbasis[...], residual, (((1,), (1,)), ((), ())), precision=HIGHEST, preferred_element_type=jnp.float32
        )
        y[pl.ds(s, lat, 2), :] = turned

    def spread(k, src_of, dst, mine):
        ss, rs = ssem.at[k], rsem.at[k]

        def put(t, b):
            pltpu.make_async_remote_copy(
                src_ref=src_of(t, b), dst_ref=dst, send_sem=ss, recv_sem=rs, device_id=(t, b), device_id_type=MESH
            ).start()

        pltpu.make_async_copy(src_of(tm, band), dst, rs).start()
        put(tm, other)

        def body(i, carry):
            t = wrap(tm + i, n)
            put(t, band)
            put(t, other)
            return carry

        lax.fori_loop(1, n, body, 0)

    spread(0, lambda t, b: y.at[pl.ds(4 * t + 2 * b, 2)], r.at[band, pl.ds(2 * tm, 2)], None)

    lam_c = lamv[pl.ds(me, 1), :]
    chunk = 32

    def evaluate(i, carry):
        at = pl.ds(pl.multiple_of(i * chunk, chunk), chunk)
        lam_r = lams[at, :]
        shift = jnp.concatenate([lam_r + lam_c] * 2, axis=1)
        mu = weights[0:1, :] - shift
        direction = jnp.broadcast_to(weights[1:2, :], mu.shape)
        remaining = jnp.ones_like(mu)
        accum = jnp.zeros_like(mu)
        for step in range(ORDER):
            accum = accum + direction
            if step < ORDER - 1:
                remaining = remaining - mu * direction
                direction = weights[2 + 2 * step : 3 + 2 * step, :] * direction + weights[3 + 2 * step : 4 + 2 * step, :] * remaining
        poly[at, :] = relaxation * accum
        return carry

    lax.fori_loop(0, lat // chunk, evaluate, 0)
    pltpu.make_async_copy(r, r, rsem.at[0]).wait()

    def dot(a, b, ca, cb):
        return lax.dot_general(a, b, (((ca,), (cb,)), ((), ())), precision=HIGHEST, preferred_element_type=jnp.float32)

    spectrum = dot(sbasis[...], jnp.concatenate([r[0], r[1]], axis=1), 1, 1)
    spectrum = dot(spectrum, tbasis[...], 1, 1) * poly[...]
    timed = dot(spectrum, tbasis[...], 1, 0)
    timed = dot(timed, sbasis[...], 0, 0)
    v[0] = timed[:, :rows]
    v[1] = timed[:, rows:]
    spread(1, lambda t, b: v.at[b, pl.ds(2 * t, 2)], w.at[pl.ds(2 * me, 2)], None)
    pltpu.make_async_copy(w, w, rsem.at[1]).wait()

    halo2 = []

    def send2(j, src, dst, device):
        halo2.append(send(j, src, dst, device))

    for s in range(2):
        value = guess[s] + dot(w[pl.ds(s, lat, 2), :], sbasis[...], 0, 0)
        sol[s, own, :] = value
        sol_out[s] = value
        if s == 0:
            send2(11, sol.at[0, own], sol.at[2, own], (before, band))
            send2(12, sol.at[0, last], sol.at[2, low], (before, other))
            send2(13, sol.at[0, first], sol.at[2, high], (before, other))
    send2(14, sol.at[both, last], sol.at[both, low], (tm, other))
    send2(15, sol.at[both, first], sol.at[both, high], (tm, other))
    halo[10].wait_recv()
    for copy in halo2:
        copy.wait_recv()

    for s in range(2):
        applied = pairs(expo[1 + s] * sol[s], ahead)
        image = (sol[1] if s == 0 else sign_after * sol[2]) - applied
        pulled = pairs(image, back)[inner]
        fermion = (-2.0 * coupling) * expo[1 + s, own, :] * sol[s, own, :] * pulled
        here = phonon[s]
        boson = stiffness * (2.0 * here - ext[0, s, own, :] - ext[0, s + 2, own, :]) + mass_term * here
        mom_out[s] = momentum[s] - step_size * (boson + fermion)

    for copy in halo + halo2:
        copy.wait_send()
    for k in range(2):
        sent = w.at[pl.ds(0, 2 * (2 * n - 1))]
        pltpu.make_async_copy(sent, sent, ssem.at[k]).wait()


def shards(n, phonon, momentum, source, guess, bonds):
    slices, rows, lat = phonon.shape
    sbasis, lam = space_basis(lat)
    tbasis = time_basis(slices * n)
    weights = cheb_tables(slices * n)
    lams = np.ascontiguousarray(np.broadcast_to(lam.astype(np.float32)[:, None], (lat, 128)))
    vmem = pl.BlockSpec(memory_space=pltpu.VMEM)
    total = rows + 2 * PAD
    f32 = jnp.float32
    return pl.pallas_call(
        functools.partial(kernel, n),
        out_shape=[jax.ShapeDtypeStruct(phonon.shape, f32)] * 2,
        in_specs=[vmem] * 10,
        out_specs=[vmem] * 2,
        scratch_shapes=[
            pltpu.VMEM((2, 4, total, lat), f32),
            pltpu.VMEM((2, total, lat), jnp.int32),
            pltpu.VMEM((8, total, lat), f32),
            pltpu.VMEM((3, total, lat), f32),
            pltpu.VMEM((lat, lat), f32),
            pltpu.VMEM((2 * lat, rows), f32),
            pltpu.VMEM((2, slices * n, rows), f32),
            pltpu.VMEM((2, slices * n, rows), f32),
            pltpu.VMEM((2 * lat, rows), f32),
            pltpu.VMEM((3, total, lat), f32),
            pltpu.SemaphoreType.DMA((2,)),
            pltpu.SemaphoreType.DMA((2,)),
            pltpu.SemaphoreType.DMA((16,)),
            pltpu.SemaphoreType.DMA((16,)),
            pltpu.SemaphoreType.DMA,
        ],
        compiler_params=pltpu.CompilerParams(
            collective_id=0, has_side_effects=True, vmem_limit_bytes=32 * 1024 * 1024
        ),
        cost_estimate=pl.CostEstimate(flops=400000000, bytes_accessed=3000000, transcendentals=200000),
    )(phonon, momentum, source, guess, bonds, jnp.asarray(tbasis), jnp.asarray(sbasis), jnp.asarray(weights), jnp.asarray(lams), jnp.asarray(lams))


def solution(mesh):
    spec = P("tm", "band", None)
    return jax.shard_map(
        functools.partial(shards, mesh.shape["tm"]),
        mesh=mesh,
        in_specs=(spec, spec, spec, spec, P(None, "band", None)),
        out_specs=(spec, spec),
        check_vma=False,
    )
```

```python
import functools
import math

import jax
import jax.numpy as jnp
import numpy as np
from jax import lax
from jax.experimental import pallas as pl
from jax.experimental.pallas import tpu as pltpu
from jax.sharding import PartitionSpec as P

ORDER = 24
hop_angle = 0.3
coupling = 0.2
stiffness = 1.0
mass_term = 0.5
relaxation = 0.25
step_size = 0.25
cheb_base = 4.03
cheb_slope = 0.5
half_width = 4.0

STRIDE = 1
MESH = pl.DeviceIdType.MESH
HIGHEST = lax.Precision.HIGHEST
PAD = 8
COSH = math.cosh(hop_angle)
SINH = math.sinh(hop_angle)


def time_basis(length):
    k = np.arange(length)[:, None]
    l = np.arange(length)[None, :]
    angle = ((2 * (k // 2) + 1) * l % (2 * length)) * (math.pi / length)
    return (math.sqrt(2.0 / length) * np.where(k % 2 == 0, np.cos(angle), np.sin(angle))).astype(np.float32)


def space_basis(length):
    k = np.arange(length)
    m = (k + 1) // 2
    angle = (m[:, None] * np.arange(length)[None, :] % length) * (2.0 * math.pi / length)
    basis = np.where((k % 2 == 1)[:, None], np.cos(angle), np.sin(angle)) * math.sqrt(2.0 / length)
    basis[0] = 1.0 / math.sqrt(length)
    basis[-1] = np.where(np.arange(length) % 2 == 0, 1.0, -1.0) / math.sqrt(length)
    return basis.astype(np.float32), (2.0 * np.cos(2.0 * math.pi * m / length))


def cheb_tables(length):
    m = np.arange(length) // 2
    centre = cheb_base + cheb_slope * (1.0 - np.cos((2 * m + 1) * math.pi / length))
    ratio = centre / half_width
    rows = [centre, 1.0 / centre]
    weight = 1.0 / ratio
    for _ in range(ORDER - 1):
        new = 1.0 / (2.0 * ratio - weight)
        rows += [new * weight, 2.0 * new / half_width]
        weight = new
    while len(rows) % 8:
        rows.append(np.zeros(length))
    return np.stack(rows).astype(np.float32)


def wrap(value, size):
    return jnp.where(value >= size, value - size, value)


def kernel(
    n, phonon_in, momentum_in, source_in, guess_in, bonds_in, tbasis_in, sbasis_in, weights_in, lams_in, sol_out, mom_out,
    source, momentum, tbasis, sbasis, weights, lams,
    ext, bond_ext, tables, expo, poly, y, r, v, w, sol, ssem, rsem, hs, hr, loads, far,
):
    rows, lat = source.shape[1:]
    total = rows + 2 * PAD
    tm, band = lax.axis_index("tm"), lax.axis_index("band")
    other = 1 - band
    me = 2 * tm + band
    after = wrap(tm + 1, n)
    before = jnp.where(tm == 0, n - 1, tm - 1)
    own = pl.ds(PAD, rows)
    both = pl.ds(0, 2)

    def load(j, src, dst):
        copy = pltpu.make_async_copy(src, dst, loads.at[j])
        copy.start()
        return copy

    load_first = [
        load(0, guess_in, ext.at[1, pl.ds(1, 2), own]),
        load(1, phonon_in, ext.at[0, pl.ds(1, 2), own]),
        load(2, bonds_in, bond_ext.at[both, own]),
    ]

    near = 8
    count = n // near
    row, col = tm // near, tm % near
    barrier = pltpu.get_barrier_semaphore()

    def signal(sem, t, b):
        pl.semaphore_signal(sem, inc=1, device_id=(t, b), device_id_type=MESH)

    def far_signals(sem):
        for i in range(1, count):
            signal(sem, wrap(row + i, count) * near + col, band)

    for t in (after, before):
        signal(barrier, t, band)
        signal(barrier, t, other)
    signal(barrier, tm, other)
    for i in range(1, near):
        t = row * near + wrap(col + i, near)
        signal(barrier, t, band)
        signal(barrier, t, other)
    far_signals(barrier)
    load_later = [
        load(3, source_in, source),
        load(4, sbasis_in, sbasis),
        load(5, tbasis_in, tbasis),
        load(6, weights_in, weights),
        load(7, lams_in, lams),
        load(8, momentum_in, momentum),
    ]
    for copy in load_first:
        copy.wait()
    pl.semaphore_wait(barrier, 5 + 2 * (near - 1) + count - 1)
    low, high = pl.ds(PAD - 2, 2), pl.ds(PAD + rows, 2)
    first, last = pl.ds(PAD, 2), pl.ds(PAD + rows - 2, 2)

    def send(j, src, dst, device):
        copy = pltpu.make_async_remote_copy(
            src_ref=src, dst_ref=dst, send_sem=hs.at[j], recv_sem=hr.at[j], device_id=device, device_id_type=MESH
        )
        copy.start()
        return copy

    halo = [
        send(0, ext.at[both, 2, own], ext.at[both, 0, own], (after, band)),
        send(1, ext.at[1, 1, own], ext.at[1, 3, own], (before, band)),
        send(2, ext.at[both, pl.ds(1, 2), last], ext.at[both, pl.ds(1, 2), low], (tm, other)),
        send(3, ext.at[both, pl.ds(1, 2), first], ext.at[both, pl.ds(1, 2), high], (tm, other)),
        send(4, bond_ext.at[both, last], bond_ext.at[both, low], (tm, other)),
        send(5, bond_ext.at[both, first], bond_ext.at[both, high], (tm, other)),
        send(6, ext.at[both, 2, last], ext.at[both, 0, low], (after, other)),
        send(7, ext.at[both, 2, first], ext.at[both, 0, high], (after, other)),
        send(8, ext.at[1, 1, last], ext.at[1, 3, low], (before, other)),
        send(9, ext.at[1, 1, first], ext.at[1, 3, high], (before, other)),
        send(10, ext.at[0, 1, own], ext.at[0, 3, own], (before, band)),
    ]
    far_signals(far)
    for copy in halo[:10]:
        copy.wait_recv()
    row_even = lax.broadcasted_iota(jnp.int32, (total, lat), 0) % 2 == 0
    col_even = lax.broadcasted_iota(jnp.int32, (total, lat), 1) % 2 == 0

    def rolled(value, by, axis):
        return pltpu.roll(value, by % value.shape[axis], axis)

    horizontal, vertical = bond_ext[0], bond_ext[1]
    left, up = rolled(horizontal, 1, 1), rolled(vertical, 1, 0)
    strengths = (
        jnp.where(col_even, horizontal, left),
        jnp.where(col_even, left, horizontal),
        jnp.where(row_even, vertical, up),
        jnp.where(row_even, up, vertical),
    )
    for q, s in enumerate(strengths):
        tables[2 * q] = jnp.where(s == 1, COSH, 1.0).astype(jnp.float32)
        tables[2 * q + 1] = jnp.where(s == 1, SINH, 0.0).astype(jnp.float32)

    def pairs(value, colours):
        for q in colours:
            axis, even = (1, col_even) if q < 2 else (0, row_even)
            plus, minus = rolled(value, -1, axis), rolled(value, 1, axis)
            partner = jnp.where(even, plus, minus) if q % 2 == 0 else jnp.where(even, minus, plus)
            value = tables[2 * q] * value + tables[2 * q + 1] * partner
        return value

    ahead = (0, 1, 2, 3)
    back = (3, 2, 1, 0)
    sign_before = jnp.where(tm == 0, -1.0, 1.0).astype(jnp.float32)
    sign_after = jnp.where(tm == n - 1, -1.0, 1.0).astype(jnp.float32)

    for s in range(3):
        expo[s] = jnp.exp(-coupling * ext[0, s])

    for copy in load_later[:2]:
        copy.wait()
    inner = slice(PAD, PAD + rows)
    link_own = ext[1, 1, own, :] - pairs(expo[0] * (sign_before * ext[1, 0]), ahead)[inner]
    for s in range(2):
        applied = pairs(expo[1 + s] * ext[1, 1 + s], ahead)
        link = (ext[1, 2] if s == 0 else sign_after * ext[1, 3]) - applied
        pulled = pairs(link, back)[inner]
        residual = source[s] - (link_own - expo[1 + s, own, :] * pulled)
        link_own = link[inner]
        turned = lax.dot_general(
            sbasis[...], residual, (((1,), (1,)), ((), ())), precision=HIGHEST, preferred_element_type=jnp.float32
        )
        y[pl.ds(s, lat, 2), :] = turned

    pl.semaphore_wait(far, count - 1)
    def spread(k, src_of, dst):
        ss, rs = ssem.at[k], rsem.at[k]

        def put(t, b):
            pltpu.make_async_remote_copy(
                src_ref=src_of(t, b), dst_ref=dst, send_sem=ss, recv_sem=rs, device_id=(t, b), device_id_type=MESH
            ).start()

        pltpu.make_async_copy(src_of(tm, band), dst, rs).start()
        put(tm, other)

        def body(i, carry):
            t = wrap(tm + carry, n)
            put(t, band)
            put(t, other)
            return wrap(carry + STRIDE, n)

        lax.fori_loop(1, n, body, STRIDE)

    spread(0, lambda t, b: y.at[pl.ds(4 * t + 2 * b, 2)], r.at[band, pl.ds(2 * tm, 2)])

    for copy in load_later[2:]:
        copy.wait()
    lam_c = lams[pl.ds(me, 1), :]
    chunk = 32

    def evaluate(i, carry):
        at = pl.ds(pl.multiple_of(i * chunk, chunk), chunk)
        lam_r = lams[at, :]
        shift = jnp.concatenate([lam_r + lam_c] * 2, axis=1)
        mu = weights[0:1, :] - shift
        direction = jnp.broadcast_to(weights[1:2, :], mu.shape)
        remaining = jnp.ones_like(mu)
        accum = jnp.zeros_like(mu)
        for step in range(ORDER):
            accum = accum + direction
            if step < ORDER - 1:
                remaining = remaining - mu * direction
                direction = weights[2 + 2 * step : 3 + 2 * step, :] * direction + weights[3 + 2 * step : 4 + 2 * step, :] * remaining
        poly[at, :] = relaxation * accum
        return carry

    lax.fori_loop(0, lat // chunk, evaluate, 0)
    pltpu.make_async_copy(r, r, rsem.at[0]).wait()

    def dot(a, b, ca, cb):
        return lax.dot_general(a, b, (((ca,), (cb,)), ((), ())), precision=HIGHEST, preferred_element_type=jnp.float32)

    spectrum = dot(sbasis[...], jnp.concatenate([r[0], r[1]], axis=1), 1, 1)
    spectrum = dot(spectrum, tbasis[...], 1, 1) * poly[...]
    timed = dot(spectrum, tbasis[...], 1, 0)
    timed = dot(timed, sbasis[...], 0, 0)
    v[0] = timed[:, :rows]
    v[1] = timed[:, rows:]
    spread(1, lambda t, b: v.at[b, pl.ds(2 * t, 2)], w.at[pl.ds(2 * me, 2)])
    pltpu.make_async_copy(w, w, rsem.at[1]).wait()

    halo2 = []

    def send2(j, src, dst, device):
        halo2.append(send(j, src, dst, device))

    for s in range(2):
        value = ext[1, 1 + s, own, :] + dot(w[pl.ds(s, lat, 2), :], sbasis[...], 0, 0)
        sol[s, own, :] = value
        sol_out[s] = value
        if s == 0:
            send2(11, sol.at[0, own], sol.at[2, own], (before, band))
            send2(12, sol.at[0, last], sol.at[2, low], (before, other))
            send2(13, sol.at[0, first], sol.at[2, high], (before, other))
    send2(14, sol.at[both, last], sol.at[both, low], (tm, other))
    send2(15, sol.at[both, first], sol.at[both, high], (tm, other))
    halo[10].wait_recv()
    for copy in halo2:
        copy.wait_recv()

    for s in range(2):
        applied = pairs(expo[1 + s] * sol[s], ahead)
        image = (sol[1] if s == 0 else sign_after * sol[2]) - applied
        pulled = pairs(image, back)[inner]
        fermion = (-2.0 * coupling) * expo[1 + s, own, :] * sol[s, own, :] * pulled
        here = ext[0, 1 + s, own, :]
        boson = stiffness * (2.0 * here - ext[0, s, own, :] - ext[0, s + 2, own, :]) + mass_term * here
        mom_out[s] = momentum[s] - step_size * (boson + fermion)

    for copy in halo + halo2:
        copy.wait_send()
    for k in range(2):
        sent = w.at[pl.ds(0, 2 * (2 * n - 1))]
        pltpu.make_async_copy(sent, sent, ssem.at[k]).wait()


def shards(n, phonon, momentum, source, guess, bonds):
    slices, rows, lat = phonon.shape
    sbasis, lam = space_basis(lat)
    tbasis = time_basis(slices * n)
    weights = cheb_tables(slices * n)
    lams = np.ascontiguousarray(np.broadcast_to(lam.astype(np.float32)[:, None], (lat, 128)))
    vmem = pl.BlockSpec(memory_space=pltpu.VMEM)
    hbm = pl.BlockSpec(memory_space=pltpu.HBM)
    total = rows + 2 * PAD
    f32 = jnp.float32
    return pl.pallas_call(
        functools.partial(kernel, n),
        out_shape=[jax.ShapeDtypeStruct(phonon.shape, f32)] * 2,
        in_specs=[hbm] * 9,
        out_specs=[vmem] * 2,
        scratch_shapes=[
            pltpu.VMEM(phonon.shape, f32),
            pltpu.VMEM(phonon.shape, f32),
            pltpu.VMEM(tbasis.shape, f32),
            pltpu.VMEM(sbasis.shape, f32),
            pltpu.VMEM(weights.shape, f32),
            pltpu.VMEM(lams.shape, f32),
            pltpu.VMEM((2, 4, total, lat), f32),
            pltpu.VMEM((2, total, lat), jnp.int32),
            pltpu.VMEM((8, total, lat), f32),
            pltpu.VMEM((3, total, lat), f32),
            pltpu.VMEM((lat, lat), f32),
            pltpu.VMEM((2 * lat, rows), f32),
            pltpu.VMEM((2, slices * n, rows), f32),
            pltpu.VMEM((2, slices * n, rows), f32),
            pltpu.VMEM((2 * lat, rows), f32),
            pltpu.VMEM((3, total, lat), f32),
            pltpu.SemaphoreType.DMA((2,)),
            pltpu.SemaphoreType.DMA((2,)),
            pltpu.SemaphoreType.DMA((16,)),
            pltpu.SemaphoreType.DMA((16,)),
            pltpu.SemaphoreType.DMA((9,)),
            pltpu.SemaphoreType.REGULAR,
        ],
        compiler_params=pltpu.CompilerParams(
            collective_id=0, has_side_effects=True, vmem_limit_bytes=63 * 1024 * 1024
        ),
        cost_estimate=pl.CostEstimate(flops=400000000, bytes_accessed=3000000, transcendentals=200000),
    )(phonon, momentum, source, guess, bonds, jnp.asarray(tbasis), jnp.asarray(sbasis), jnp.asarray(weights), jnp.asarray(lams))


def solution(mesh):
    spec = P("tm", "band")
    return jax.shard_map(
        functools.partial(shards, mesh.shape["tm"]),
        mesh=mesh,
        in_specs=(spec, spec, spec, spec, P(None, "band", None)),
        out_specs=(spec, spec),
        check_vma=False,
    )
```

```python
import functools
import math

import jax
import jax.numpy as jnp
import numpy as np
from jax import lax
from jax.experimental import pallas as pl
from jax.experimental.pallas import tpu as pltpu
from jax.sharding import PartitionSpec as P

ORDER = 24
hop_angle = 0.3
coupling = 0.2
stiffness = 1.0
mass_term = 0.5
relaxation = 0.25
step_size = 0.25
cheb_base = 4.03
cheb_slope = 0.5
half_width = 4.0

MESH = pl.DeviceIdType.MESH
PAD = 8
COSH = math.cosh(hop_angle)
SINH = math.sinh(hop_angle)


def time_basis(length):
    k = np.arange(length)[:, None]
    l = np.arange(length)[None, :]
    angle = ((2 * (k // 2) + 1) * l % (2 * length)) * (math.pi / length)
    return (math.sqrt(2.0 / length) * np.where(k % 2 == 0, np.cos(angle), np.sin(angle))).astype(np.float32)


def space_basis(length):
    k = np.arange(length)
    m = (k + 1) // 2
    angle = (m[:, None] * np.arange(length)[None, :] % length) * (2.0 * math.pi / length)
    basis = np.where((k % 2 == 1)[:, None], np.cos(angle), np.sin(angle)) * math.sqrt(2.0 / length)
    basis[0] = 1.0 / math.sqrt(length)
    basis[-1] = np.where(np.arange(length) % 2 == 0, 1.0, -1.0) / math.sqrt(length)
    return basis.astype(np.float32), (2.0 * np.cos(2.0 * math.pi * m / length))


def cheb_tables(length):
    m = np.arange(length) // 2
    centre = cheb_base + cheb_slope * (1.0 - np.cos((2 * m + 1) * math.pi / length))
    ratio = centre / half_width
    rows = [centre, 1.0 / centre]
    weight = 1.0 / ratio
    for _ in range(ORDER - 1):
        new = 1.0 / (2.0 * ratio - weight)
        rows += [new * weight, 2.0 * new / half_width]
        weight = new
    while len(rows) % 8:
        rows.append(np.zeros(length))
    return np.stack(rows).astype(np.float32)


def wrap(value, size):
    return jnp.where(value >= size, value - size, value)


def halves(value):
    top = value.astype(jnp.bfloat16)
    return top, (value - top.astype(jnp.float32)).astype(jnp.bfloat16)


def dot(a, b, ca, cb):
    dims = (((ca,), (cb,)), ((), ()))

    def one(p, q):
        return lax.dot_general(p, q, dims, preferred_element_type=jnp.float32)

    return one(a[0], b[0]) + (one(a[0], b[1]) + one(a[1], b[0]))


def kernel(
    n, phonon_in, momentum_in, source_in, guess_in, bonds_in, tbasis_in, sbasis_in, weights_in, lams_in, sol_out, mom_out,
    source, momentum, tbasis, sbasis, weights, lams,
    ext, bond_ext, tables, expo, app, app_in, app_edge, edge_out, phonon_prev, poly, y, r, v, w, sol, new,
    ssem, rsem, hs, hr, loads, far,
):
    rows, lat = source.shape[1:]
    total = rows + 2 * PAD
    tm, band = lax.axis_index("tm"), lax.axis_index("band")
    other = 1 - band
    me = 2 * tm + band
    after = wrap(tm + 1, n)
    before = jnp.where(tm == 0, n - 1, tm - 1)
    own = pl.ds(PAD, rows)
    both = pl.ds(0, 2)

    def load(j, src, dst):
        copy = pltpu.make_async_copy(src, dst, loads.at[j])
        copy.start()
        return copy

    load_first = [
        load(0, guess_in, ext.at[1, both, own]),
        load(1, phonon_in, ext.at[0, both, own]),
        load(2, bonds_in, bond_ext.at[both, own]),
    ]

    near = 8
    count = n // near
    row, col = tm // near, tm % near
    barrier = pltpu.get_barrier_semaphore()

    def signal(sem, t, b):
        pl.semaphore_signal(sem, inc=1, device_id=(t, b), device_id_type=MESH)

    def far_signals(sem):
        for i in range(1, count):
            signal(sem, wrap(row + i, count) * near + col, band)

    for t in (after, before):
        signal(barrier, t, band)
        signal(barrier, t, other)
    signal(barrier, tm, other)
    for i in range(1, near):
        t = row * near + wrap(col + i, near)
        signal(barrier, t, band)
        signal(barrier, t, other)
    far_signals(barrier)
    load_later = [
        load(3, source_in, source),
        load(4, sbasis_in, sbasis),
        load(5, tbasis_in, tbasis),
        load(6, weights_in, weights),
        load(7, lams_in, lams),
        load(8, momentum_in, momentum),
    ]
    for copy in load_first:
        copy.wait()
    pl.semaphore_wait(barrier, 5 + 2 * (near - 1) + count - 1)
    low, high = pl.ds(PAD - 2, 2), pl.ds(PAD + rows, 2)
    first, last = pl.ds(PAD, 2), pl.ds(PAD + rows - 2, 2)
    started = []

    def send(j, src, dst, device):
        copy = pltpu.make_async_remote_copy(
            src_ref=src, dst_ref=dst, send_sem=hs.at[j], recv_sem=hr.at[j], device_id=device, device_id_type=MESH
        )
        copy.start()
        started.append(copy)
        return copy

    edges = [
        send(1, ext.at[both, both, last], ext.at[both, both, low], (tm, other)),
        send(2, ext.at[both, both, first], ext.at[both, both, high], (tm, other)),
        send(3, bond_ext.at[both, last], bond_ext.at[both, low], (tm, other)),
        send(4, bond_ext.at[both, first], bond_ext.at[both, high], (tm, other)),
    ]
    next_guess = [
        send(0, ext.at[1, 0, own], ext.at[1, 2, own], (before, band)),
        send(5, ext.at[1, 0, last], ext.at[1, 2, low], (before, other)),
        send(6, ext.at[1, 0, first], ext.at[1, 2, high], (before, other)),
    ]

    def parity(size, axis):
        return lax.broadcasted_iota(jnp.int32, (size, lat), axis) % 2 == 0

    def rolled(value, by, axis):
        return pltpu.roll(value, by % value.shape[axis], axis)

    def make_tables(at, size, keep):
        row_even, col_even = parity(size, 0), parity(size, 1)
        horizontal, vertical = bond_ext[0, at : at + size, :], bond_ext[1, at : at + size, :]
        left, up = rolled(horizontal, 1, 1), rolled(vertical, 1, 0)
        strengths = (
            jnp.where(col_even, horizontal, left),
            jnp.where(col_even, left, horizontal),
            jnp.where(row_even, vertical, up),
            jnp.where(row_even, up, vertical),
        )
        begin, end = keep
        for q, s in enumerate(strengths):
            s = s[begin:end]
            tables[2 * q, at + begin : at + end, :] = jnp.where(s == 1, COSH, 1.0).astype(jnp.float32)
            tables[2 * q + 1, at + begin : at + end, :] = jnp.where(s == 1, SINH, 0.0).astype(jnp.float32)

    def pairs(value, colours, at):
        size = value.shape[0]
        row_even, col_even = parity(size, 0), parity(size, 1)
        for q in colours:
            axis, even = (1, col_even) if q < 2 else (0, row_even)
            plus, minus = rolled(value, -1, axis), rolled(value, 1, axis)
            partner = jnp.where(even, plus, minus) if q % 2 == 0 else jnp.where(even, minus, plus)
            value = tables[2 * q, at : at + size, :] * value + tables[2 * q + 1, at : at + size, :] * partner
        return value

    ahead = (0, 1, 2, 3)
    back = (3, 2, 1, 0)
    sign_before = jnp.where(tm == 0, -1.0, 1.0).astype(jnp.float32)
    sign_after = jnp.where(tm == n - 1, -1.0, 1.0).astype(jnp.float32)
    end = PAD + rows

    make_tables(PAD, rows, (0, rows))
    for s in (1, 0):
        expo[s, own, :] = jnp.exp(-coupling * ext[0, s, own, :])
        app[s, own, :] = pairs(expo[s, own, :] * ext[1, s, own, :], ahead, PAD)
        if s == 1:
            bulk = send(7, app.at[1, pl.ds(2 * PAD, rows - 2 * PAD)], app_in.at[pl.ds(PAD, rows - 2 * PAD)], (after, band))
    far_signals(far)
    for copy in edges:
        copy.wait_recv()
    make_tables(0, 2 * PAD, (0, 2 * PAD))
    make_tables(end - PAD, 2 * PAD, (PAD, 2 * PAD))
    tile = lax.broadcasted_iota(jnp.int32, (PAD, lat), 0)
    for s in (1, 0):
        for outer, block in ((0, 0), (end, end - PAD)):
            expo[s, outer : outer + PAD, :] = jnp.exp(-coupling * ext[0, s, outer : outer + PAD, :])
            here = slice(block, block + 2 * PAD)
            fixed = pairs(expo[s, here, :] * ext[1, s, here, :], ahead, block)
            if outer == 0:
                app[s, 0:PAD, :] = fixed[:PAD]
                mixed = jnp.where(tile == 0, fixed[PAD:], app[s, PAD : 2 * PAD, :])
                app[s, PAD : 2 * PAD, :] = mixed
            else:
                app[s, end : end + PAD, :] = fixed[PAD:]
                mixed = jnp.where(tile == PAD - 1, fixed[:PAD], app[s, end - PAD : end, :])
                app[s, end - PAD : end, :] = mixed
            if s == 1:
                edge_out[0 if outer == 0 else 1] = mixed
        if s == 1:
            edge_sent = send(8, edge_out, app_edge, (after, band))

    inner = slice(PAD, end)
    link = ext[1, 1] - app[0]
    pulled = pairs(link, back, 0)[inner]
    for copy in load_later[:2]:
        copy.wait()
    space = halves(sbasis[...])
    half = source[0] - ext[1, 0, own, :] + expo[0, own, :] * pulled
    link_own = link[inner]
    for copy in next_guess:
        copy.wait_recv()
    pulled = pairs(sign_after * ext[1, 2] - app[1], back, 0)[inner]
    residual = source[1] - (link_own - expo[1, own, :] * pulled)
    y[pl.ds(1, lat, 2), :] = dot(space, halves(residual), 1, 1)
    bulk.wait_recv()
    edge_sent.wait_recv()
    app_in[0:PAD, :] = app_edge[0]
    app_in[rows - PAD : rows, :] = app_edge[1]
    y[pl.ds(0, lat, 2), :] = dot(space, halves(half + sign_before * app_in[...]), 1, 1)

    pl.semaphore_wait(far, count - 1)
    def spread(k, src_of, dst):
        ss, rs = ssem.at[k], rsem.at[k]

        def put(t, b):
            pltpu.make_async_remote_copy(
                src_ref=src_of(t, b), dst_ref=dst, send_sem=ss, recv_sem=rs, device_id=(t, b), device_id_type=MESH
            ).start()

        pltpu.make_async_copy(src_of(tm, band), dst, rs).start()
        put(tm, other)

        def body(i, carry):
            t = wrap(tm + i, n)
            put(t, band)
            put(t, other)
            return carry

        lax.fori_loop(1, n, body, 0)

    spread(0, lambda t, b: y.at[pl.ds(4 * t + 2 * b, 2)], r.at[band, pl.ds(2 * tm, 2)])

    for copy in load_later[2:]:
        copy.wait()
    lam_c = lams[pl.ds(me, 1), :]
    chunk = 32

    def evaluate(i, carry):
        at = pl.ds(pl.multiple_of(i * chunk, chunk), chunk)
        lam_r = lams[at, :]
        shift = jnp.concatenate([lam_r + lam_c] * 2, axis=1)
        mu = weights[0:1, :] - shift
        direction = jnp.broadcast_to(weights[1:2, :], mu.shape)
        remaining = jnp.ones_like(mu)
        accum = jnp.zeros_like(mu)
        for step in range(ORDER):
            accum = accum + direction
            if step < ORDER - 1:
                remaining = remaining - mu * direction
                direction = weights[2 + 2 * step : 3 + 2 * step, :] * direction + weights[3 + 2 * step : 4 + 2 * step, :] * remaining
        poly[at, :] = relaxation * accum
        return carry

    lax.fori_loop(0, lat // chunk, evaluate, 0)
    slots = halves(tbasis[...])
    pltpu.make_async_copy(r, r, rsem.at[0]).wait()
    phonons = [
        send(9, ext.at[0, 1, own], phonon_prev, (after, band)),
        send(10, ext.at[0, 0, own], ext.at[0, 2, own], (before, band)),
    ]
    spectrum = dot(space, halves(jnp.concatenate([r[0], r[1]], axis=1)), 1, 1)
    spectrum = dot(halves(spectrum), slots, 1, 1) * poly[...]
    timed = dot(halves(spectrum), slots, 1, 0)
    timed = dot(halves(timed), space, 0, 0)
    v[0] = timed[:, :rows]
    v[1] = timed[:, rows:]
    spread(1, lambda t, b: v.at[b, pl.ds(2 * t, 2)], w.at[pl.ds(2 * me, 2)])
    for copy in phonons:
        copy.wait_recv()
    for s in range(2):
        here = ext[0, s, own, :]
        one_before = phonon_prev[...] if s == 0 else ext[0, 0, own, :]
        boson = stiffness * (2.0 * here - one_before - ext[0, s + 1, own, :]) + mass_term * here
        momentum[s] = momentum[s] - step_size * boson
    pltpu.make_async_copy(w, w, rsem.at[1]).wait()
    next_sol = []
    for s in range(2):
        sol[s, own, :] = ext[1, s, own, :] + dot(halves(w[pl.ds(s, lat, 2), :]), space, 0, 0)
        if s == 0:
            next_sol.append(send(11, sol.at[0, own], sol.at[2, own], (before, band)))
            next_sol.append(send(12, sol.at[0, last], sol.at[2, low], (before, other)))
            next_sol.append(send(13, sol.at[0, first], sol.at[2, high], (before, other)))
    sol_edges = [
        send(14, sol.at[both, last], sol.at[both, low], (tm, other)),
        send(15, sol.at[both, first], sol.at[both, high], (tm, other)),
    ]
    written = [load(0, sol.at[both, own], sol_out)]
    for copy in sol_edges:
        copy.wait_recv()
    applied = [pairs(expo[s] * sol[s], ahead, 0) for s in range(2)]
    for s in range(2):
        if s == 1:
            for copy in next_sol:
                copy.wait_recv()
        image = (sol[1] if s == 0 else sign_after * sol[2]) - applied[s]
        pulled = pairs(image, back, 0)[inner]
        fermion = (-2.0 * coupling) * expo[s, own, :] * sol[s, own, :] * pulled
        new[s] = momentum[s] - step_size * fermion
        written.append(load(1 + s, new.at[s], mom_out.at[s]))

    for copy in started:
        copy.wait_send()
    for k in range(2):
        sent = w.at[pl.ds(0, 2 * (2 * n - 1))]
        pltpu.make_async_copy(sent, sent, ssem.at[k]).wait()
    for copy in written:
        copy.wait()


def finish(sol_in, mom_in, sol_out, mom_out, held, sems):
    pieces = []
    for i, (src, dst) in enumerate(((sol_in, sol_out), (mom_in, mom_out))):
        for s in range(2):
            j = 2 * i + s
            pieces.append(
                (
                    pltpu.make_async_copy(src.at[s], held.at[j], sems.at[0, j]),
                    pltpu.make_async_copy(held.at[j], dst.at[s], sems.at[1, j]),
                )
            )
    for fetch, _ in pieces:
        fetch.start()
    for fetch, store in pieces:
        fetch.wait()
        store.start()
    for _, store in pieces:
        store.wait()


def shards(n, phonon, momentum, source, guess, bonds):
    slices, rows, lat = phonon.shape
    sbasis, lam = space_basis(lat)
    tbasis = time_basis(slices * n)
    weights = cheb_tables(slices * n)
    lams = np.ascontiguousarray(np.broadcast_to(lam.astype(np.float32)[:, None], (lat, 128)))
    hbm = pl.BlockSpec(memory_space=pltpu.HBM)
    total = rows + 2 * PAD
    f32 = jnp.float32
    made = pl.pallas_call(
        functools.partial(kernel, n),
        out_shape=[jax.ShapeDtypeStruct(phonon.shape, f32)] * 2,
        in_specs=[hbm] * 9,
        out_specs=[hbm] * 2,
        scratch_shapes=[
            pltpu.VMEM(phonon.shape, f32),
            pltpu.VMEM(phonon.shape, f32),
            pltpu.VMEM(tbasis.shape, f32),
            pltpu.VMEM(sbasis.shape, f32),
            pltpu.VMEM(weights.shape, f32),
            pltpu.VMEM(lams.shape, f32),
            pltpu.VMEM((2, 3, total, lat), f32),
            pltpu.VMEM((2, total, lat), jnp.int32),
            pltpu.VMEM((8, total, lat), f32),
            pltpu.VMEM((2, total, lat), f32),
            pltpu.VMEM((2, total, lat), f32),
            pltpu.VMEM((rows, lat), f32),
            pltpu.VMEM((2, PAD, lat), f32),
            pltpu.VMEM((2, PAD, lat), f32),
            pltpu.VMEM((rows, lat), f32),
            pltpu.VMEM((lat, lat), f32),
            pltpu.VMEM((2 * lat, rows), f32),
            pltpu.VMEM((2, slices * n, rows), f32),
            pltpu.VMEM((2, slices * n, rows), f32),
            pltpu.VMEM((2 * lat, rows), f32),
            pltpu.VMEM((3, total, lat), f32),
            pltpu.VMEM(phonon.shape, f32),
            pltpu.SemaphoreType.DMA((2,)),
            pltpu.SemaphoreType.DMA((2,)),
            pltpu.SemaphoreType.DMA((16,)),
            pltpu.SemaphoreType.DMA((16,)),
            pltpu.SemaphoreType.DMA((9,)),
            pltpu.SemaphoreType.REGULAR,
        ],
        compiler_params=pltpu.CompilerParams(
            collective_id=0, has_side_effects=True, vmem_limit_bytes=63 * 1024 * 1024
        ),
        cost_estimate=pl.CostEstimate(flops=400000000, bytes_accessed=3000000, transcendentals=200000),
    )(phonon, momentum, source, guess, bonds, jnp.asarray(tbasis), jnp.asarray(sbasis), jnp.asarray(weights), jnp.asarray(lams))
    return pl.pallas_call(
        finish,
        out_shape=[jax.ShapeDtypeStruct(phonon.shape, f32)] * 2,
        in_specs=[hbm] * 2,
        out_specs=[hbm] * 2,
        scratch_shapes=[pltpu.VMEM((4, rows, lat), f32), pltpu.SemaphoreType.DMA((2, 4))],
        compiler_params=pltpu.CompilerParams(vmem_limit_bytes=63 * 1024 * 1024),
        cost_estimate=pl.CostEstimate(flops=0, bytes_accessed=1048576, transcendentals=0),
    )(*made)


def solution(mesh):
    spec = P("tm", "band")
    return jax.shard_map(
        functools.partial(shards, mesh.shape["tm"]),
        mesh=mesh,
        in_specs=(spec, spec, spec, spec, P(None, "band", None)),
        out_specs=(spec, spec),
        check_vma=False,
    )
```

```python
import functools
import math

import jax
import jax.numpy as jnp
import numpy as np
from jax import lax
from jax.experimental import pallas as pl
from jax.experimental.pallas import tpu as pltpu
from jax.sharding import PartitionSpec as P

ORDER = 24
hop_angle = 0.3
coupling = 0.2
stiffness = 1.0
mass_term = 0.5
relaxation = 0.25
step_size = 0.25
cheb_base = 4.03
cheb_slope = 0.5
half_width = 4.0

MESH = pl.DeviceIdType.MESH
PAD = 8
COSH = math.cosh(hop_angle)
SINH = math.sinh(hop_angle)


def time_basis(length):
    k = np.arange(length)[:, None]
    l = np.arange(length)[None, :]
    angle = ((2 * (k // 2) + 1) * l % (2 * length)) * (math.pi / length)
    return (math.sqrt(2.0 / length) * np.where(k % 2 == 0, np.cos(angle), np.sin(angle))).astype(np.float32)


def space_basis(length):
    k = np.arange(length)
    m = (k + 1) // 2
    angle = (m[:, None] * np.arange(length)[None, :] % length) * (2.0 * math.pi / length)
    basis = np.where((k % 2 == 1)[:, None], np.cos(angle), np.sin(angle)) * math.sqrt(2.0 / length)
    basis[0] = 1.0 / math.sqrt(length)
    basis[-1] = np.where(np.arange(length) % 2 == 0, 1.0, -1.0) / math.sqrt(length)
    return basis.astype(np.float32), (2.0 * np.cos(2.0 * math.pi * m / length))


def cheb_tables(length):
    m = np.arange(length) // 2
    centre = cheb_base + cheb_slope * (1.0 - np.cos((2 * m + 1) * math.pi / length))
    ratio = centre / half_width
    rows = [centre, 1.0 / centre]
    weight = 1.0 / ratio
    for _ in range(ORDER - 1):
        new = 1.0 / (2.0 * ratio - weight)
        rows += [new * weight, 2.0 * new / half_width]
        weight = new
    while len(rows) % 8:
        rows.append(np.zeros(length))
    return np.stack(rows).astype(np.float32)


def wrap(value, size):
    return jnp.where(value >= size, value - size, value)


def halves(value):
    top = value.astype(jnp.bfloat16)
    return top, (value - top.astype(jnp.float32)).astype(jnp.bfloat16)


def dot(a, b, ca, cb):
    dims = (((ca,), (cb,)), ((), ()))

    def one(p, q):
        return lax.dot_general(p, q, dims, preferred_element_type=jnp.float32)

    return one(a[0], b[0]) + (one(a[0], b[1]) + one(a[1], b[0]))


def kernel(
    n, phonon_in, momentum_in, source_in, guess_in, bonds_in, consts_in, sol_out, mom_out,
    source, momentum, consts,
    ext, bond_ext, tables, expo, app, app_in, app_edge, edge_out, phonon_prev, poly, y, r, v, w, sol,
    ssem, rsem, hs, hr, loads, far,
):
    rows, lat = source.shape[1:]
    total = rows + 2 * PAD
    tm, band = lax.axis_index("tm"), lax.axis_index("band")
    other = 1 - band
    me = 2 * tm + band
    after = wrap(tm + 1, n)
    before = jnp.where(tm == 0, n - 1, tm - 1)
    tbasis, sbasis = consts.at[0:lat], consts.at[lat : 2 * lat]
    lams, weights = consts.at[2 * lat : 3 * lat], consts.at[3 * lat : 3 * lat + 48]
    own = pl.ds(PAD, rows)
    both = pl.ds(0, 2)

    def load(j, src, dst):
        copy = pltpu.make_async_copy(src, dst, loads.at[j])
        copy.start()
        return copy

    load_first = [
        load(0, guess_in, ext.at[1, both, own]),
        load(1, phonon_in, ext.at[0, both, own]),
        load(2, bonds_in, bond_ext.at[both, own]),
    ]

    near = 8
    count = n // near
    row, col = tm // near, tm % near
    barrier = pltpu.get_barrier_semaphore()

    def signal(sem, t, b):
        pl.semaphore_signal(sem, inc=1, device_id=(t, b), device_id_type=MESH)

    def far_signals(sem):
        for i in range(1, count):
            signal(sem, wrap(row + i, count) * near + col, band)

    for t in (after, before):
        signal(barrier, t, band)
        signal(barrier, t, other)
    signal(barrier, tm, other)
    for i in range(1, near):
        t = row * near + wrap(col + i, near)
        signal(barrier, t, band)
        signal(barrier, t, other)
    far_signals(barrier)
    load_later = [
        load(3, source_in, source),
        load(4, consts_in, consts),
        load(5, momentum_in, momentum),
    ]
    for copy in load_first:
        copy.wait()
    pl.semaphore_wait(barrier, 5 + 2 * (near - 1) + count - 1)
    low, high = pl.ds(PAD - 2, 2), pl.ds(PAD + rows, 2)
    first, last = pl.ds(PAD, 2), pl.ds(PAD + rows - 2, 2)
    started = []

    def send(j, src, dst, device):
        copy = pltpu.make_async_remote_copy(
            src_ref=src, dst_ref=dst, send_sem=hs.at[j], recv_sem=hr.at[j], device_id=device, device_id_type=MESH
        )
        copy.start()
        started.append(copy)
        return copy

    edges = [
        send(1, ext.at[both, both, last], ext.at[both, both, low], (tm, other)),
        send(2, ext.at[both, both, first], ext.at[both, both, high], (tm, other)),
        send(3, bond_ext.at[both, last], bond_ext.at[both, low], (tm, other)),
        send(4, bond_ext.at[both, first], bond_ext.at[both, high], (tm, other)),
    ]
    next_guess = [
        send(0, ext.at[1, 0, own], ext.at[1, 2, own], (before, band)),
        send(5, ext.at[1, 0, last], ext.at[1, 2, low], (before, other)),
        send(6, ext.at[1, 0, first], ext.at[1, 2, high], (before, other)),
    ]

    def parity(size, axis):
        return lax.broadcasted_iota(jnp.int32, (size, lat), axis) % 2 == 0

    def rolled(value, by, axis):
        return pltpu.roll(value, by % value.shape[axis], axis)

    def make_tables(at, size, keep):
        row_even, col_even = parity(size, 0), parity(size, 1)
        horizontal, vertical = bond_ext[0, at : at + size, :], bond_ext[1, at : at + size, :]
        left, up = rolled(horizontal, 1, 1), rolled(vertical, 1, 0)
        strengths = (
            jnp.where(col_even, horizontal, left),
            jnp.where(col_even, left, horizontal),
            jnp.where(row_even, vertical, up),
            jnp.where(row_even, up, vertical),
        )
        begin, end = keep
        for q, s in enumerate(strengths):
            s = s[begin:end]
            tables[2 * q, at + begin : at + end, :] = jnp.where(s == 1, COSH, 1.0).astype(jnp.float32)
            tables[2 * q + 1, at + begin : at + end, :] = jnp.where(s == 1, SINH, 0.0).astype(jnp.float32)

    def pairs(value, colours, at):
        size = value.shape[0]
        row_even, col_even = parity(size, 0), parity(size, 1)
        for q in colours:
            axis, even = (1, col_even) if q < 2 else (0, row_even)
            plus, minus = rolled(value, -1, axis), rolled(value, 1, axis)
            partner = jnp.where(even, plus, minus) if q % 2 == 0 else jnp.where(even, minus, plus)
            value = tables[2 * q, at : at + size, :] * value + tables[2 * q + 1, at : at + size, :] * partner
        return value

    ahead = (0, 1, 2, 3)
    back = (3, 2, 1, 0)
    sign_before = jnp.where(tm == 0, -1.0, 1.0).astype(jnp.float32)
    sign_after = jnp.where(tm == n - 1, -1.0, 1.0).astype(jnp.float32)
    end = PAD + rows

    make_tables(PAD, rows, (0, rows))
    for s in (1, 0):
        expo[s, own, :] = jnp.exp(-coupling * ext[0, s, own, :])
        app[s, own, :] = pairs(expo[s, own, :] * ext[1, s, own, :], ahead, PAD)
        if s == 1:
            bulk = send(7, app.at[1, pl.ds(2 * PAD, rows - 2 * PAD)], app_in.at[pl.ds(PAD, rows - 2 * PAD)], (after, band))
    far_signals(far)
    for copy in edges:
        copy.wait_recv()
    make_tables(0, 2 * PAD, (0, 2 * PAD))
    make_tables(end - PAD, 2 * PAD, (PAD, 2 * PAD))
    tile = lax.broadcasted_iota(jnp.int32, (PAD, lat), 0)
    for s in (1, 0):
        for outer, block in ((0, 0), (end, end - PAD)):
            expo[s, outer : outer + PAD, :] = jnp.exp(-coupling * ext[0, s, outer : outer + PAD, :])
            here = slice(block, block + 2 * PAD)
            fixed = pairs(expo[s, here, :] * ext[1, s, here, :], ahead, block)
            if outer == 0:
                app[s, 0:PAD, :] = fixed[:PAD]
                mixed = jnp.where(tile == 0, fixed[PAD:], app[s, PAD : 2 * PAD, :])
                app[s, PAD : 2 * PAD, :] = mixed
            else:
                app[s, end : end + PAD, :] = fixed[PAD:]
                mixed = jnp.where(tile == PAD - 1, fixed[:PAD], app[s, end - PAD : end, :])
                app[s, end - PAD : end, :] = mixed
            if s == 1:
                edge_out[0 if outer == 0 else 1] = mixed
        if s == 1:
            edge_sent = send(8, edge_out, app_edge, (after, band))

    inner = slice(PAD, end)
    link = ext[1, 1] - app[0]
    pulled = pairs(link, back, 0)[inner]
    for copy in load_later[:2]:
        copy.wait()
    space = halves(sbasis[...])
    half = source[0] - ext[1, 0, own, :] + expo[0, own, :] * pulled
    link_own = link[inner]
    for copy in next_guess:
        copy.wait_recv()
    pulled = pairs(sign_after * ext[1, 2] - app[1], back, 0)[inner]
    residual = source[1] - (link_own - expo[1, own, :] * pulled)
    y[pl.ds(1, lat, 2), :] = dot(space, halves(residual), 1, 1)
    bulk.wait_recv()
    edge_sent.wait_recv()
    app_in[0:PAD, :] = app_edge[0]
    app_in[rows - PAD : rows, :] = app_edge[1]
    y[pl.ds(0, lat, 2), :] = dot(space, halves(half + sign_before * app_in[...]), 1, 1)

    pl.semaphore_wait(far, count - 1)
    def spread(k, src_of, dst):
        ss, rs = ssem.at[k], rsem.at[k]

        def put(t, b):
            pltpu.make_async_remote_copy(
                src_ref=src_of(t, b), dst_ref=dst, send_sem=ss, recv_sem=rs, device_id=(t, b), device_id_type=MESH
            ).start()

        pltpu.make_async_copy(src_of(tm, band), dst, rs).start()
        put(tm, other)

        def body(i, carry):
            t = wrap(tm + i, n)
            put(t, band)
            put(t, other)
            return carry

        lax.fori_loop(1, n, body, 0)

    spread(0, lambda t, b: y.at[pl.ds(4 * t + 2 * b, 2)], r.at[band, pl.ds(2 * tm, 2)])

    for copy in load_later[2:]:
        copy.wait()
    lam_c = lams[pl.ds(me, 1), :]
    chunk = 32

    def evaluate(i, carry):
        at = pl.ds(pl.multiple_of(i * chunk, chunk), chunk)
        lam_r = lams[at, :]
        mu = weights[0:1, :] - (lam_r + lam_c)
        direction = jnp.broadcast_to(weights[1:2, :], mu.shape)
        remaining = jnp.ones_like(mu)
        accum = jnp.zeros_like(mu)
        for step in range(ORDER):
            accum = accum + direction
            if step < ORDER - 1:
                remaining = remaining - mu * direction
                direction = weights[2 + 2 * step : 3 + 2 * step, :] * direction + weights[3 + 2 * step : 4 + 2 * step, :] * remaining
        poly[at, :] = relaxation * accum
        return carry

    lax.fori_loop(0, lat // chunk, evaluate, 0)
    slots = halves(tbasis[...])
    pltpu.make_async_copy(r, r, rsem.at[0]).wait()
    phonons = [
        send(9, ext.at[0, 1, own], phonon_prev, (after, band)),
        send(10, ext.at[0, 0, own], ext.at[0, 2, own], (before, band)),
    ]
    spectrum = dot(space, halves(jnp.concatenate([r[0], r[1]], axis=1)), 1, 1)
    spectrum = dot(halves(spectrum), slots, 1, 1) * poly[...]
    timed = dot(halves(spectrum), slots, 1, 0)
    timed = dot(halves(timed), space, 0, 0)
    v[0] = timed[:, :rows]
    v[1] = timed[:, rows:]
    spread(1, lambda t, b: v.at[b, pl.ds(2 * t, 2)], w.at[pl.ds(2 * me, 2)])
    for copy in phonons:
        copy.wait_recv()
    for s in range(2):
        here = ext[0, s, own, :]
        one_before = phonon_prev[...] if s == 0 else ext[0, 0, own, :]
        boson = stiffness * (2.0 * here - one_before - ext[0, s + 1, own, :]) + mass_term * here
        momentum[s] = momentum[s] - step_size * boson
    pltpu.make_async_copy(w, w, rsem.at[1]).wait()
    next_sol = []
    for s in range(2):
        value = ext[1, s, own, :] + dot(halves(w[pl.ds(s, lat, 2), :]), space, 0, 0)
        sol[s, own, :] = value
        sol_out[s] = value
        if s == 0:
            next_sol.append(send(11, sol.at[0, own], sol.at[2, own], (before, band)))
            next_sol.append(send(12, sol.at[0, last], sol.at[2, low], (before, other)))
            next_sol.append(send(13, sol.at[0, first], sol.at[2, high], (before, other)))
    sol_edges = [
        send(14, sol.at[both, last], sol.at[both, low], (tm, other)),
        send(15, sol.at[both, first], sol.at[both, high], (tm, other)),
    ]
    for copy in sol_edges:
        copy.wait_recv()
    applied = [pairs(expo[s] * sol[s], ahead, 0) for s in range(2)]
    for s in range(2):
        if s == 1:
            for copy in next_sol:
                copy.wait_recv()
        image = (sol[1] if s == 0 else sign_after * sol[2]) - applied[s]
        pulled = pairs(image, back, 0)[inner]
        fermion = (-2.0 * coupling) * expo[s, own, :] * sol[s, own, :] * pulled
        mom_out[s] = momentum[s] - step_size * fermion

    for copy in started:
        copy.wait_send()
    for k in range(2):
        sent = w.at[pl.ds(0, 2 * (2 * n - 1))]
        pltpu.make_async_copy(sent, sent, ssem.at[k]).wait()


def finish(sol_in, mom_in, sol_out, mom_out, sems):
    copies = [
        pltpu.make_async_copy(src.at[s], dst.at[s], sems.at[i, s])
        for i, (src, dst) in enumerate(((sol_in, sol_out), (mom_in, mom_out)))
        for s in range(2)
    ]
    for copy in copies:
        copy.start()
    for copy in copies:
        copy.wait()


def shards(n, phonon, momentum, source, guess, bonds):
    slices, rows, lat = phonon.shape
    sbasis, lam = space_basis(lat)
    tbasis = time_basis(slices * n)
    weights = cheb_tables(slices * n)
    lams = np.broadcast_to(lam.astype(np.float32)[:, None], (lat, lat))
    consts = np.concatenate([tbasis, sbasis, lams, weights])
    vmem = pl.BlockSpec(memory_space=pltpu.VMEM)
    hbm = pl.BlockSpec(memory_space=pltpu.HBM)
    total = rows + 2 * PAD
    f32 = jnp.float32
    made = pl.pallas_call(
        functools.partial(kernel, n),
        out_shape=[jax.ShapeDtypeStruct(phonon.shape, f32)] * 2,
        in_specs=[hbm] * 6,
        out_specs=[vmem] * 2,
        scratch_shapes=[
            pltpu.VMEM(phonon.shape, f32),
            pltpu.VMEM(phonon.shape, f32),
            pltpu.VMEM(consts.shape, f32),
            pltpu.VMEM((2, 3, total, lat), f32),
            pltpu.VMEM((2, total, lat), jnp.int32),
            pltpu.VMEM((8, total, lat), f32),
            pltpu.VMEM((2, total, lat), f32),
            pltpu.VMEM((2, total, lat), f32),
            pltpu.VMEM((rows, lat), f32),
            pltpu.VMEM((2, PAD, lat), f32),
            pltpu.VMEM((2, PAD, lat), f32),
            pltpu.VMEM((rows, lat), f32),
            pltpu.VMEM((lat, lat), f32),
            pltpu.VMEM((2 * lat, rows), f32),
            pltpu.VMEM((2, slices * n, rows), f32),
            pltpu.VMEM((2, slices * n, rows), f32),
            pltpu.VMEM((2 * lat, rows), f32),
            pltpu.VMEM((3, total, lat), f32),
            pltpu.SemaphoreType.DMA((2,)),
            pltpu.SemaphoreType.DMA((2,)),
            pltpu.SemaphoreType.DMA((16,)),
            pltpu.SemaphoreType.DMA((16,)),
            pltpu.SemaphoreType.DMA((6,)),
            pltpu.SemaphoreType.REGULAR,
        ],
        compiler_params=pltpu.CompilerParams(
            collective_id=0, has_side_effects=True, vmem_limit_bytes=(53 * 1024 + 256) * 1024
        ),
        cost_estimate=pl.CostEstimate(flops=400000000, bytes_accessed=3000000, transcendentals=200000),
    )(phonon, momentum, source, guess, bonds, jnp.asarray(consts))
    return pl.pallas_call(
        finish,
        out_shape=[jax.ShapeDtypeStruct(phonon.shape, f32)] * 2,
        in_specs=[vmem] * 2,
        out_specs=[hbm] * 2,
        scratch_shapes=[pltpu.SemaphoreType.DMA((2, 2))],
        compiler_params=pltpu.CompilerParams(vmem_limit_bytes=8 * 1024 * 1024),
        cost_estimate=pl.CostEstimate(flops=0, bytes_accessed=1048576, transcendentals=0),
    )(*made)


def solution(mesh):
    spec = P("tm", "band")
    return jax.shard_map(
        functools.partial(shards, mesh.shape["tm"]),
        mesh=mesh,
        in_specs=(spec, spec, spec, spec, P(None, "band", None)),
        out_specs=(spec, spec),
        check_vma=False,
    )
```

```python
import functools
import math

import jax
import jax.numpy as jnp
import numpy as np
from jax import lax
from jax.experimental import pallas as pl
from jax.experimental.pallas import tpu as pltpu
from jax.sharding import PartitionSpec as P

ORDER = 24
hop_angle = 0.3
coupling = 0.2
stiffness = 1.0
mass_term = 0.5
relaxation = 0.25
step_size = 0.25
cheb_base = 4.03
cheb_slope = 0.5
half_width = 4.0

MESH = pl.DeviceIdType.MESH
PAD = 8
COSH = math.cosh(hop_angle)
SINH = math.sinh(hop_angle)


def time_basis(length):
    k = np.arange(length)[:, None]
    l = np.arange(length)[None, :]
    angle = ((2 * (k // 2) + 1) * l % (2 * length)) * (math.pi / length)
    return (math.sqrt(2.0 / length) * np.where(k % 2 == 0, np.cos(angle), np.sin(angle))).astype(np.float32)


def space_basis(length):
    k = np.arange(length)
    m = (k + 1) // 2
    angle = (m[:, None] * np.arange(length)[None, :] % length) * (2.0 * math.pi / length)
    basis = np.where((k % 2 == 1)[:, None], np.cos(angle), np.sin(angle)) * math.sqrt(2.0 / length)
    basis[0] = 1.0 / math.sqrt(length)
    basis[-1] = np.where(np.arange(length) % 2 == 0, 1.0, -1.0) / math.sqrt(length)
    return basis.astype(np.float32), (2.0 * np.cos(2.0 * math.pi * m / length))


def cheb_tables(length):
    m = np.arange(length) // 2
    centre = cheb_base + cheb_slope * (1.0 - np.cos((2 * m + 1) * math.pi / length))
    ratio = centre / half_width
    rows = [centre, 1.0 / centre]
    weight = 1.0 / ratio
    for _ in range(ORDER - 1):
        new = 1.0 / (2.0 * ratio - weight)
        rows += [new * weight, 2.0 * new / half_width]
        weight = new
    while len(rows) % 8:
        rows.append(np.zeros(length))
    return np.stack(rows).astype(np.float32)


def wrap(value, size):
    return jnp.where(value >= size, value - size, value)


def halves(value):
    top = value.astype(jnp.bfloat16)
    return top, (value - top.astype(jnp.float32)).astype(jnp.bfloat16)


def dot(a, b, ca, cb):
    dims = (((ca,), (cb,)), ((), ()))

    def one(p, q):
        return lax.dot_general(p, q, dims, preferred_element_type=jnp.float32)

    return one(a[0], b[0]) + (one(a[0], b[1]) + one(a[1], b[0]))


def kernel(
    n, phonon_in, momentum_in, source_in, guess_in, bonds_in, consts_in, sol_out, mom_out,
    source, momentum, consts,
    ext, bond_ext, tables, expo, app, app_in, app_edge, edge_out, phonon_prev, poly, y, r, v, w, sol,
    ssem, rsem, hs, hr, loads, far,
):
    rows, lat = source.shape[1:]
    total = rows + 2 * PAD
    tm, band = lax.axis_index("tm"), lax.axis_index("band")
    other = 1 - band
    me = 2 * tm + band
    after = wrap(tm + 1, n)
    before = jnp.where(tm == 0, n - 1, tm - 1)
    tbasis, sbasis = consts.at[0:lat], consts.at[lat : 2 * lat]
    lams, weights = consts.at[2 * lat : 3 * lat], consts.at[3 * lat : 3 * lat + 48]
    own = pl.ds(PAD, rows)
    both = pl.ds(0, 2)

    def load(j, src, dst):
        copy = pltpu.make_async_copy(src, dst, loads.at[j])
        copy.start()
        return copy

    load_first = [
        load(0, guess_in, ext.at[1, both, own]),
        load(1, phonon_in, ext.at[0, both, own]),
        load(2, bonds_in, bond_ext.at[both, own]),
    ]

    near = 8
    count = n // near
    row, col = tm // near, tm % near
    barrier = pltpu.get_barrier_semaphore()

    def signal(sem, t, b):
        pl.semaphore_signal(sem, inc=1, device_id=(t, b), device_id_type=MESH)

    def far_signals(sem):
        for i in range(1, count):
            signal(sem, wrap(row + i, count) * near + col, band)

    for t in (after, before):
        signal(barrier, t, band)
        signal(barrier, t, other)
    signal(barrier, tm, other)
    for i in range(1, near):
        t = row * near + wrap(col + i, near)
        signal(barrier, t, band)
        signal(barrier, t, other)
    far_signals(barrier)
    load_later = [
        load(3, source_in, source),
        load(4, consts_in, consts),
        load(5, momentum_in, momentum),
    ]
    for copy in load_first:
        copy.wait()
    pl.semaphore_wait(barrier, 5 + 2 * (near - 1) + count - 1)
    low, high = pl.ds(PAD - 2, 2), pl.ds(PAD + rows, 2)
    first, last = pl.ds(PAD, 2), pl.ds(PAD + rows - 2, 2)
    started = []

    def send(j, src, dst, device):
        copy = pltpu.make_async_remote_copy(
            src_ref=src, dst_ref=dst, send_sem=hs.at[j], recv_sem=hr.at[j], device_id=device, device_id_type=MESH
        )
        copy.start()
        started.append(copy)
        return copy

    edges = [
        send(1, ext.at[both, both, last], ext.at[both, both, low], (tm, other)),
        send(2, ext.at[both, both, first], ext.at[both, both, high], (tm, other)),
        send(3, bond_ext.at[both, last], bond_ext.at[both, low], (tm, other)),
        send(4, bond_ext.at[both, first], bond_ext.at[both, high], (tm, other)),
    ]
    next_guess = [
        send(0, ext.at[1, 0, own], ext.at[1, 2, own], (before, band)),
        send(5, ext.at[1, 0, last], ext.at[1, 2, low], (before, other)),
        send(6, ext.at[1, 0, first], ext.at[1, 2, high], (before, other)),
    ]

    def parity(size, axis):
        return lax.broadcasted_iota(jnp.int32, (size, lat), axis) % 2 == 0

    def rolled(value, by, axis):
        return pltpu.roll(value, by % value.shape[axis], axis)

    def make_tables(at, size, keep):
        row_even, col_even = parity(size, 0), parity(size, 1)
        horizontal, vertical = bond_ext[0, at : at + size, :], bond_ext[1, at : at + size, :]
        left, up = rolled(horizontal, 1, 1), rolled(vertical, 1, 0)
        strengths = (
            jnp.where(col_even, horizontal, left),
            jnp.where(col_even, left, horizontal),
            jnp.where(row_even, vertical, up),
            jnp.where(row_even, up, vertical),
        )
        begin, end = keep
        for q, s in enumerate(strengths):
            s = s[begin:end]
            tables[2 * q, at + begin : at + end, :] = jnp.where(s == 1, COSH, 1.0).astype(jnp.float32)
            tables[2 * q + 1, at + begin : at + end, :] = jnp.where(s == 1, SINH, 0.0).astype(jnp.float32)

    def pairs(value, colours, at):
        size = value.shape[0]
        row_even, col_even = parity(size, 0), parity(size, 1)
        for q in colours:
            axis, even = (1, col_even) if q < 2 else (0, row_even)
            plus, minus = rolled(value, -1, axis), rolled(value, 1, axis)
            partner = jnp.where(even, plus, minus) if q % 2 == 0 else jnp.where(even, minus, plus)
            value = tables[2 * q, at : at + size, :] * value + tables[2 * q + 1, at : at + size, :] * partner
        return value

    ahead = (0, 1, 2, 3)
    back = (3, 2, 1, 0)
    sign_before = jnp.where(tm == 0, -1.0, 1.0).astype(jnp.float32)
    sign_after = jnp.where(tm == n - 1, -1.0, 1.0).astype(jnp.float32)
    end = PAD + rows

    make_tables(PAD, rows, (0, rows))
    for s in (1, 0):
        expo[s, own, :] = jnp.exp(-coupling * ext[0, s, own, :])
        app[s, own, :] = pairs(expo[s, own, :] * ext[1, s, own, :], ahead, PAD)
        if s == 1:
            bulk = send(7, app.at[1, pl.ds(2 * PAD, rows - 2 * PAD)], app_in.at[pl.ds(PAD, rows - 2 * PAD)], (after, band))
    far_signals(far)
    for copy in edges:
        copy.wait_recv()
    make_tables(0, 2 * PAD, (0, 2 * PAD))
    make_tables(end - PAD, 2 * PAD, (PAD, 2 * PAD))
    tile = lax.broadcasted_iota(jnp.int32, (PAD, lat), 0)
    for s in (1, 0):
        for outer, block in ((0, 0), (end, end - PAD)):
            expo[s, outer : outer + PAD, :] = jnp.exp(-coupling * ext[0, s, outer : outer + PAD, :])
            here = slice(block, block + 2 * PAD)
            fixed = pairs(expo[s, here, :] * ext[1, s, here, :], ahead, block)
            if outer == 0:
                app[s, 0:PAD, :] = fixed[:PAD]
                mixed = jnp.where(tile == 0, fixed[PAD:], app[s, PAD : 2 * PAD, :])
                app[s, PAD : 2 * PAD, :] = mixed
            else:
                app[s, end : end + PAD, :] = fixed[PAD:]
                mixed = jnp.where(tile == PAD - 1, fixed[:PAD], app[s, end - PAD : end, :])
                app[s, end - PAD : end, :] = mixed
            if s == 1:
                edge_out[0 if outer == 0 else 1] = mixed
        if s == 1:
            edge_sent = send(8, edge_out, app_edge, (after, band))

    inner = slice(PAD, end)
    link = ext[1, 1] - app[0]
    pulled = pairs(link, back, 0)[inner]
    for copy in load_later[:2]:
        copy.wait()
    space = halves(sbasis[...])
    half = source[0] - ext[1, 0, own, :] + expo[0, own, :] * pulled
    link_own = link[inner]
    for copy in next_guess:
        copy.wait_recv()
    pulled = pairs(sign_after * ext[1, 2] - app[1], back, 0)[inner]
    residual = source[1] - (link_own - expo[1, own, :] * pulled)
    y[pl.ds(1, lat, 2), :] = dot(space, halves(residual), 1, 1)
    bulk.wait_recv()
    edge_sent.wait_recv()
    app_in[0:PAD, :] = app_edge[0]
    app_in[rows - PAD : rows, :] = app_edge[1]
    y[pl.ds(0, lat, 2), :] = dot(space, halves(half + sign_before * app_in[...]), 1, 1)

    pl.semaphore_wait(far, count - 1)
    def spread(k, src_of, dst):
        ss, rs = ssem.at[k], rsem.at[k]

        def put(t, b):
            pltpu.make_async_remote_copy(
                src_ref=src_of(t, b), dst_ref=dst, send_sem=ss, recv_sem=rs, device_id=(t, b), device_id_type=MESH
            ).start()

        pltpu.make_async_copy(src_of(tm, band), dst, rs).start()
        put(tm, other)

        def body(i, carry):
            t = wrap(tm + i, n)
            put(t, band)
            put(t, other)
            return carry

        lax.fori_loop(1, n, body, 0, unroll=4)

    spread(0, lambda t, b: y.at[pl.ds(4 * t + 2 * b, 2)], r.at[band, pl.ds(2 * tm, 2)])

    for copy in load_later[2:]:
        copy.wait()
    lam_c = lams[pl.ds(me, 1), :]
    chunk = 32

    def evaluate(i, carry):
        at = pl.ds(pl.multiple_of(i * chunk, chunk), chunk)
        lam_r = lams[at, :]
        mu = weights[0:1, :] - (lam_r + lam_c)
        direction = jnp.broadcast_to(weights[1:2, :], mu.shape)
        remaining = jnp.ones_like(mu)
        accum = jnp.zeros_like(mu)
        for step in range(ORDER):
            accum = accum + direction
            if step < ORDER - 1:
                remaining = remaining - mu * direction
                direction = weights[2 + 2 * step : 3 + 2 * step, :] * direction + weights[3 + 2 * step : 4 + 2 * step, :] * remaining
        poly[at, :] = relaxation * accum
        return carry

    lax.fori_loop(0, lat // chunk, evaluate, 0)
    slots = halves(tbasis[...])
    pltpu.make_async_copy(r, r, rsem.at[0]).wait()
    phonons = [
        send(9, ext.at[0, 1, own], phonon_prev, (after, band)),
        send(10, ext.at[0, 0, own], ext.at[0, 2, own], (before, band)),
    ]
    spectrum = dot(space, halves(jnp.concatenate([r[0], r[1]], axis=1)), 1, 1)
    spectrum = dot(halves(spectrum), slots, 1, 1) * poly[...]
    timed = dot(halves(spectrum), slots, 1, 0)
    timed = dot(halves(timed), space, 0, 0)
    v[0] = timed[:, :rows]
    v[1] = timed[:, rows:]
    spread(1, lambda t, b: v.at[b, pl.ds(2 * t, 2)], w.at[pl.ds(2 * me, 2)])
    for copy in phonons:
        copy.wait_recv()
    for s in range(2):
        here = ext[0, s, own, :]
        one_before = phonon_prev[...] if s == 0 else ext[0, 0, own, :]
        boson = stiffness * (2.0 * here - one_before - ext[0, s + 1, own, :]) + mass_term * here
        momentum[s] = momentum[s] - step_size * boson
    pltpu.make_async_copy(w, w, rsem.at[1]).wait()
    next_sol = []
    for s in range(2):
        value = ext[1, s, own, :] + dot(halves(w[pl.ds(s, lat, 2), :]), space, 0, 0)
        sol[s, own, :] = value
        sol_out[s] = value
        if s == 0:
            next_sol.append(send(11, sol.at[0, own], sol.at[2, own], (before, band)))
            next_sol.append(send(12, sol.at[0, last], sol.at[2, low], (before, other)))
            next_sol.append(send(13, sol.at[0, first], sol.at[2, high], (before, other)))
    sol_edges = [
        send(14, sol.at[both, last], sol.at[both, low], (tm, other)),
        send(15, sol.at[both, first], sol.at[both, high], (tm, other)),
    ]
    for copy in sol_edges:
        copy.wait_recv()
    applied = [pairs(expo[s] * sol[s], ahead, 0) for s in range(2)]
    for s in range(2):
        if s == 1:
            for copy in next_sol:
                copy.wait_recv()
        image = (sol[1] if s == 0 else sign_after * sol[2]) - applied[s]
        pulled = pairs(image, back, 0)[inner]
        fermion = (-2.0 * coupling) * expo[s, own, :] * sol[s, own, :] * pulled
        mom_out[s] = momentum[s] - step_size * fermion

    for copy in started:
        copy.wait_send()
    for k in range(2):
        sent = w.at[pl.ds(0, 2 * (2 * n - 1))]
        pltpu.make_async_copy(sent, sent, ssem.at[k]).wait()


def finish(sol_in, mom_in, sol_out, mom_out, sems):
    copies = [
        pltpu.make_async_copy(src.at[s], dst.at[s], sems.at[i, s])
        for i, (src, dst) in enumerate(((sol_in, sol_out), (mom_in, mom_out)))
        for s in range(2)
    ]
    for copy in copies:
        copy.start()
    for copy in copies:
        copy.wait()


def shards(n, phonon, momentum, source, guess, bonds):
    slices, rows, lat = phonon.shape
    sbasis, lam = space_basis(lat)
    tbasis = time_basis(slices * n)
    weights = cheb_tables(slices * n)
    lams = np.broadcast_to(lam.astype(np.float32)[:, None], (lat, lat))
    consts = np.concatenate([tbasis, sbasis, lams, weights])
    vmem = pl.BlockSpec(memory_space=pltpu.VMEM)
    hbm = pl.BlockSpec(memory_space=pltpu.HBM)
    total = rows + 2 * PAD
    f32 = jnp.float32
    made = pl.pallas_call(
        functools.partial(kernel, n),
        out_shape=[jax.ShapeDtypeStruct(phonon.shape, f32)] * 2,
        in_specs=[hbm] * 6,
        out_specs=[vmem] * 2,
        scratch_shapes=[
            pltpu.VMEM(phonon.shape, f32),
            pltpu.VMEM(phonon.shape, f32),
            pltpu.VMEM(consts.shape, f32),
            pltpu.VMEM((2, 3, total, lat), f32),
            pltpu.VMEM((2, total, lat), jnp.int32),
            pltpu.VMEM((8, total, lat), f32),
            pltpu.VMEM((2, total, lat), f32),
            pltpu.VMEM((2, total, lat), f32),
            pltpu.VMEM((rows, lat), f32),
            pltpu.VMEM((2, PAD, lat), f32),
            pltpu.VMEM((2, PAD, lat), f32),
            pltpu.VMEM((rows, lat), f32),
            pltpu.VMEM((lat, lat), f32),
            pltpu.VMEM((2 * lat, rows), f32),
            pltpu.VMEM((2, slices * n, rows), f32),
            pltpu.VMEM((2, slices * n, rows), f32),
            pltpu.VMEM((2 * lat, rows), f32),
            pltpu.VMEM((3, total, lat), f32),
            pltpu.SemaphoreType.DMA((2,)),
            pltpu.SemaphoreType.DMA((2,)),
            pltpu.SemaphoreType.DMA((16,)),
            pltpu.SemaphoreType.DMA((16,)),
            pltpu.SemaphoreType.DMA((6,)),
            pltpu.SemaphoreType.REGULAR,
        ],
        compiler_params=pltpu.CompilerParams(
            collective_id=0, has_side_effects=True, vmem_limit_bytes=(53 * 1024 + 256) * 1024
        ),
        cost_estimate=pl.CostEstimate(flops=400000000, bytes_accessed=3000000, transcendentals=200000),
    )(phonon, momentum, source, guess, bonds, jnp.asarray(consts))
    return pl.pallas_call(
        finish,
        out_shape=[jax.ShapeDtypeStruct(phonon.shape, f32)] * 2,
        in_specs=[vmem] * 2,
        out_specs=[hbm] * 2,
        scratch_shapes=[pltpu.SemaphoreType.DMA((2, 2))],
        compiler_params=pltpu.CompilerParams(vmem_limit_bytes=8 * 1024 * 1024),
        cost_estimate=pl.CostEstimate(flops=0, bytes_accessed=1048576, transcendentals=0),
    )(*made)


def solution(mesh):
    spec = P("tm", "band")
    return jax.shard_map(
        functools.partial(shards, mesh.shape["tm"]),
        mesh=mesh,
        in_specs=(spec, spec, spec, spec, P(None, "band", None)),
        out_specs=(spec, spec),
        check_vma=False,
    )
```

```python
import functools
import math

import jax
import jax.numpy as jnp
import numpy as np
from jax import lax
from jax.experimental import pallas as pl
from jax.experimental.pallas import tpu as pltpu
from jax.sharding import PartitionSpec as P

ORDER = 24
hop_angle = 0.3
coupling = 0.2
stiffness = 1.0
mass_term = 0.5
relaxation = 0.25
step_size = 0.25
cheb_base = 4.03
cheb_slope = 0.5
half_width = 4.0

MESH = pl.DeviceIdType.MESH
PAD = 8
COSH = math.cosh(hop_angle)
SINH = math.sinh(hop_angle)


def time_basis(length):
    k = np.arange(length)[:, None]
    l = np.arange(length)[None, :]
    angle = ((2 * (k // 2) + 1) * l % (2 * length)) * (math.pi / length)
    return (math.sqrt(2.0 / length) * np.where(k % 2 == 0, np.cos(angle), np.sin(angle))).astype(np.float32)


def space_basis(length):
    k = np.arange(length)
    m = (k + 1) // 2
    angle = (m[:, None] * np.arange(length)[None, :] % length) * (2.0 * math.pi / length)
    basis = np.where((k % 2 == 1)[:, None], np.cos(angle), np.sin(angle)) * math.sqrt(2.0 / length)
    basis[0] = 1.0 / math.sqrt(length)
    basis[-1] = np.where(np.arange(length) % 2 == 0, 1.0, -1.0) / math.sqrt(length)
    return basis.astype(np.float32), (2.0 * np.cos(2.0 * math.pi * m / length))


def cheb_tables(length):
    m = np.arange(length) // 2
    centre = cheb_base + cheb_slope * (1.0 - np.cos((2 * m + 1) * math.pi / length))
    ratio = centre / half_width
    rows = [centre, 1.0 / centre]
    weight = 1.0 / ratio
    for _ in range(ORDER - 1):
        new = 1.0 / (2.0 * ratio - weight)
        rows += [new * weight, 2.0 * new / half_width]
        weight = new
    while len(rows) % 8:
        rows.append(np.zeros(length))
    return np.stack(rows).astype(np.float32)


def wrap(value, size):
    return jnp.where(value >= size, value - size, value)


def halves(value):
    top = value.astype(jnp.bfloat16)
    return top, (value - top.astype(jnp.float32)).astype(jnp.bfloat16)


def dot(a, b, ca, cb):
    dims = (((ca,), (cb,)), ((), ()))

    def one(p, q):
        return lax.dot_general(p, q, dims, preferred_element_type=jnp.float32)

    return one(a[0], b[0]) + (one(a[0], b[1]) + one(a[1], b[0]))


def kernel(
    n, phonon_in, momentum_in, source_in, guess_in, bonds_in, consts_in, sol_out, mom_out,
    source, momentum, consts,
    ext, bond_ext, tables, expo, app, app_in, app_edge, edge_out, phonon_prev, poly, y, r, v, w, sol,
    ssem, rsem, hs, hr, loads, far,
):
    rows, lat = source.shape[1:]
    total = rows + 2 * PAD
    tm, band = lax.axis_index("tm"), lax.axis_index("band")
    other = 1 - band
    me = 2 * tm + band
    after = wrap(tm + 1, n)
    before = jnp.where(tm == 0, n - 1, tm - 1)
    tbasis, sbasis = consts.at[0:lat], consts.at[lat : 2 * lat]
    lams, weights = consts.at[2 * lat : 3 * lat], consts.at[3 * lat : 3 * lat + 48]
    own = pl.ds(PAD, rows)
    both = pl.ds(0, 2)

    def load(j, src, dst):
        copy = pltpu.make_async_copy(src, dst, loads.at[j])
        copy.start()
        return copy

    load_first = [
        load(0, guess_in, ext.at[1, both, own]),
        load(1, phonon_in, ext.at[0, both, own]),
        load(2, bonds_in, bond_ext.at[both, own]),
    ]

    near = 8
    count = n // near
    row, col = tm // near, tm % near
    barrier = pltpu.get_barrier_semaphore()

    def signal(sem, t, b):
        pl.semaphore_signal(sem, inc=1, device_id=(t, b), device_id_type=MESH)

    def far_signals(sem):
        for i in range(1, count):
            signal(sem, wrap(row + i, count) * near + col, band)

    for t in (after, before):
        signal(barrier, t, band)
        signal(barrier, t, other)
    signal(barrier, tm, other)
    for i in range(1, near):
        t = row * near + wrap(col + i, near)
        signal(barrier, t, band)
        signal(barrier, t, other)
    far_signals(barrier)
    load_later = [
        load(3, source_in, source),
        load(4, consts_in, consts),
        load(5, momentum_in, momentum),
    ]
    for copy in load_first:
        copy.wait()
    pl.semaphore_wait(barrier, 5 + 2 * (near - 1) + count - 1)
    low, high = pl.ds(PAD - 2, 2), pl.ds(PAD + rows, 2)
    first, last = pl.ds(PAD, 2), pl.ds(PAD + rows - 2, 2)
    started = []

    def send(j, src, dst, device):
        copy = pltpu.make_async_remote_copy(
            src_ref=src, dst_ref=dst, send_sem=hs.at[j], recv_sem=hr.at[j], device_id=device, device_id_type=MESH
        )
        copy.start()
        started.append(copy)
        return copy

    edges = [
        send(1, ext.at[both, both, last], ext.at[both, both, low], (tm, other)),
        send(2, ext.at[both, both, first], ext.at[both, both, high], (tm, other)),
        send(3, bond_ext.at[both, last], bond_ext.at[both, low], (tm, other)),
        send(4, bond_ext.at[both, first], bond_ext.at[both, high], (tm, other)),
    ]
    next_guess = [
        send(0, ext.at[1, 0, own], ext.at[1, 2, own], (before, band)),
        send(5, ext.at[1, 0, last], ext.at[1, 2, low], (before, other)),
        send(6, ext.at[1, 0, first], ext.at[1, 2, high], (before, other)),
    ]

    def parity(size, axis):
        return lax.broadcasted_iota(jnp.int32, (size, lat), axis) % 2 == 0

    def rolled(value, by, axis):
        return pltpu.roll(value, by % value.shape[axis], axis)

    def make_tables(at, size, keep):
        row_even, col_even = parity(size, 0), parity(size, 1)
        horizontal, vertical = bond_ext[0, at : at + size, :], bond_ext[1, at : at + size, :]
        left, up = rolled(horizontal, 1, 1), rolled(vertical, 1, 0)
        strengths = (
            jnp.where(col_even, horizontal, left),
            jnp.where(col_even, left, horizontal),
            jnp.where(row_even, vertical, up),
            jnp.where(row_even, up, vertical),
        )
        begin, end = keep
        for q, s in enumerate(strengths):
            s = s[begin:end]
            tables[2 * q, at + begin : at + end, :] = jnp.where(s == 1, COSH, 1.0).astype(jnp.float32)
            tables[2 * q + 1, at + begin : at + end, :] = jnp.where(s == 1, SINH, 0.0).astype(jnp.float32)

    def pairs(value, colours, at):
        size = value.shape[0]
        row_even, col_even = parity(size, 0), parity(size, 1)
        for q in colours:
            axis, even = (1, col_even) if q < 2 else (0, row_even)
            plus, minus = rolled(value, -1, axis), rolled(value, 1, axis)
            partner = jnp.where(even, plus, minus) if q % 2 == 0 else jnp.where(even, minus, plus)
            value = tables[2 * q, at : at + size, :] * value + tables[2 * q + 1, at : at + size, :] * partner
        return value

    ahead = (0, 1, 2, 3)
    back = (3, 2, 1, 0)
    sign_before = jnp.where(tm == 0, -1.0, 1.0).astype(jnp.float32)
    sign_after = jnp.where(tm == n - 1, -1.0, 1.0).astype(jnp.float32)
    end = PAD + rows

    make_tables(PAD, rows, (0, rows))
    for s in (1, 0):
        expo[s, own, :] = jnp.exp(-coupling * ext[0, s, own, :])
        app[s, own, :] = pairs(expo[s, own, :] * ext[1, s, own, :], ahead, PAD)
        if s == 1:
            bulk = send(7, app.at[1, pl.ds(2 * PAD, rows - 2 * PAD)], app_in.at[pl.ds(PAD, rows - 2 * PAD)], (after, band))
    far_signals(far)
    for copy in edges:
        copy.wait_recv()
    make_tables(0, 2 * PAD, (0, 2 * PAD))
    make_tables(end - PAD, 2 * PAD, (PAD, 2 * PAD))
    tile = lax.broadcasted_iota(jnp.int32, (PAD, lat), 0)
    for s in (1, 0):
        for outer, block in ((0, 0), (end, end - PAD)):
            expo[s, outer : outer + PAD, :] = jnp.exp(-coupling * ext[0, s, outer : outer + PAD, :])
            here = slice(block, block + 2 * PAD)
            fixed = pairs(expo[s, here, :] * ext[1, s, here, :], ahead, block)
            if outer == 0:
                app[s, 0:PAD, :] = fixed[:PAD]
                mixed = jnp.where(tile == 0, fixed[PAD:], app[s, PAD : 2 * PAD, :])
                app[s, PAD : 2 * PAD, :] = mixed
            else:
                app[s, end : end + PAD, :] = fixed[PAD:]
                mixed = jnp.where(tile == PAD - 1, fixed[:PAD], app[s, end - PAD : end, :])
                app[s, end - PAD : end, :] = mixed
            if s == 1:
                edge_out[0 if outer == 0 else 1] = mixed
        if s == 1:
            edge_sent = send(8, edge_out, app_edge, (after, band))

    inner = slice(PAD, end)
    link = ext[1, 1] - app[0]
    pulled = pairs(link, back, 0)[inner]
    for copy in load_later[:2]:
        copy.wait()
    space = halves(sbasis[...])
    half = source[0] - ext[1, 0, own, :] + expo[0, own, :] * pulled
    link_own = link[inner]
    for copy in next_guess:
        copy.wait_recv()
    pulled = pairs(sign_after * ext[1, 2] - app[1], back, 0)[inner]
    residual = source[1] - (link_own - expo[1, own, :] * pulled)
    y[pl.ds(1, lat, 2), :] = dot(space, halves(residual), 1, 1)
    def spread(k, src_of, dst):
        ss, rs = ssem.at[k], rsem.at[k]

        def put(t, b):
            pltpu.make_async_remote_copy(
                src_ref=src_of(t, b), dst_ref=dst, send_sem=ss, recv_sem=rs, device_id=(t, b), device_id_type=MESH
            ).start()

        pltpu.make_async_copy(src_of(tm, band), dst, rs).start()
        put(tm, other)

        def body(i, carry):
            t = wrap(tm + i, n)
            put(t, band)
            put(t, other)
            return carry

        lax.fori_loop(1, n, body, 0, unroll=4)

    def part_out(s):
        spread(0, lambda t, b: y.at[pl.ds(4 * t + 2 * b + s, 1)], r.at[band, pl.ds(2 * tm + s, 1)])

    pl.semaphore_wait(far, count - 1)
    part_out(1)
    bulk.wait_recv()
    edge_sent.wait_recv()
    app_in[0:PAD, :] = app_edge[0]
    app_in[rows - PAD : rows, :] = app_edge[1]
    y[pl.ds(0, lat, 2), :] = dot(space, halves(half + sign_before * app_in[...]), 1, 1)

    part_out(0)

    for copy in load_later[2:]:
        copy.wait()
    lam_c = lams[pl.ds(me, 1), :]
    chunk = 32

    def evaluate(i, carry):
        at = pl.ds(pl.multiple_of(i * chunk, chunk), chunk)
        lam_r = lams[at, :]
        mu = weights[0:1, :] - (lam_r + lam_c)
        direction = jnp.broadcast_to(weights[1:2, :], mu.shape)
        remaining = jnp.ones_like(mu)
        accum = jnp.zeros_like(mu)
        for step in range(ORDER):
            accum = accum + direction
            if step < ORDER - 1:
                remaining = remaining - mu * direction
                direction = weights[2 + 2 * step : 3 + 2 * step, :] * direction + weights[3 + 2 * step : 4 + 2 * step, :] * remaining
        poly[at, :] = relaxation * accum
        return carry

    lax.fori_loop(0, lat // chunk, evaluate, 0)
    slots = halves(tbasis[...])
    pltpu.make_async_copy(r, r, rsem.at[0]).wait()
    phonons = [
        send(9, ext.at[0, 1, own], phonon_prev, (after, band)),
        send(10, ext.at[0, 0, own], ext.at[0, 2, own], (before, band)),
    ]
    spectrum = dot(space, halves(jnp.concatenate([r[0], r[1]], axis=1)), 1, 1)
    spectrum = dot(halves(spectrum), slots, 1, 1) * poly[...]
    timed = dot(halves(spectrum), slots, 1, 0)
    timed = dot(halves(timed), space, 0, 0)
    v[0] = timed[:, :rows]
    v[1] = timed[:, rows:]
    spread(1, lambda t, b: v.at[b, pl.ds(2 * t, 2)], w.at[pl.ds(2 * me, 2)])
    for copy in phonons:
        copy.wait_recv()
    for s in range(2):
        here = ext[0, s, own, :]
        one_before = phonon_prev[...] if s == 0 else ext[0, 0, own, :]
        boson = stiffness * (2.0 * here - one_before - ext[0, s + 1, own, :]) + mass_term * here
        momentum[s] = momentum[s] - step_size * boson
    pltpu.make_async_copy(w, w, rsem.at[1]).wait()
    next_sol = []
    for s in range(2):
        value = ext[1, s, own, :] + dot(halves(w[pl.ds(s, lat, 2), :]), space, 0, 0)
        sol[s, own, :] = value
        sol_out[s] = value
        if s == 0:
            next_sol.append(send(11, sol.at[0, own], sol.at[2, own], (before, band)))
            next_sol.append(send(12, sol.at[0, last], sol.at[2, low], (before, other)))
            next_sol.append(send(13, sol.at[0, first], sol.at[2, high], (before, other)))
    sol_edges = [
        send(14, sol.at[both, last], sol.at[both, low], (tm, other)),
        send(15, sol.at[both, first], sol.at[both, high], (tm, other)),
    ]
    for copy in sol_edges:
        copy.wait_recv()
    applied = [pairs(expo[s] * sol[s], ahead, 0) for s in range(2)]
    for s in range(2):
        if s == 1:
            for copy in next_sol:
                copy.wait_recv()
        image = (sol[1] if s == 0 else sign_after * sol[2]) - applied[s]
        pulled = pairs(image, back, 0)[inner]
        fermion = (-2.0 * coupling) * expo[s, own, :] * sol[s, own, :] * pulled
        mom_out[s] = momentum[s] - step_size * fermion

    for copy in started:
        copy.wait_send()
    for k in range(2):
        sent = w.at[pl.ds(0, 2 * (2 * n - 1))]
        pltpu.make_async_copy(sent, sent, ssem.at[k]).wait()


def finish(sol_in, mom_in, sol_out, mom_out, sems):
    copies = [
        pltpu.make_async_copy(src.at[s], dst.at[s], sems.at[i, s])
        for i, (src, dst) in enumerate(((sol_in, sol_out), (mom_in, mom_out)))
        for s in range(2)
    ]
    for copy in copies:
        copy.start()
    for copy in copies:
        copy.wait()


def shards(n, phonon, momentum, source, guess, bonds):
    slices, rows, lat = phonon.shape
    sbasis, lam = space_basis(lat)
    tbasis = time_basis(slices * n)
    weights = cheb_tables(slices * n)
    lams = np.broadcast_to(lam.astype(np.float32)[:, None], (lat, lat))
    consts = np.concatenate([tbasis, sbasis, lams, weights])
    vmem = pl.BlockSpec(memory_space=pltpu.VMEM)
    hbm = pl.BlockSpec(memory_space=pltpu.HBM)
    total = rows + 2 * PAD
    f32 = jnp.float32
    made = pl.pallas_call(
        functools.partial(kernel, n),
        out_shape=[jax.ShapeDtypeStruct(phonon.shape, f32)] * 2,
        in_specs=[hbm] * 6,
        out_specs=[vmem] * 2,
        scratch_shapes=[
            pltpu.VMEM(phonon.shape, f32),
            pltpu.VMEM(phonon.shape, f32),
            pltpu.VMEM(consts.shape, f32),
            pltpu.VMEM((2, 3, total, lat), f32),
            pltpu.VMEM((2, total, lat), jnp.int32),
            pltpu.VMEM((8, total, lat), f32),
            pltpu.VMEM((2, total, lat), f32),
            pltpu.VMEM((2, total, lat), f32),
            pltpu.VMEM((rows, lat), f32),
            pltpu.VMEM((2, PAD, lat), f32),
            pltpu.VMEM((2, PAD, lat), f32),
            pltpu.VMEM((rows, lat), f32),
            pltpu.VMEM((lat, lat), f32),
            pltpu.VMEM((2 * lat, rows), f32),
            pltpu.VMEM((2, slices * n, rows), f32),
            pltpu.VMEM((2, slices * n, rows), f32),
            pltpu.VMEM((2 * lat, rows), f32),
            pltpu.VMEM((3, total, lat), f32),
            pltpu.SemaphoreType.DMA((2,)),
            pltpu.SemaphoreType.DMA((2,)),
            pltpu.SemaphoreType.DMA((16,)),
            pltpu.SemaphoreType.DMA((16,)),
            pltpu.SemaphoreType.DMA((6,)),
            pltpu.SemaphoreType.REGULAR,
        ],
        compiler_params=pltpu.CompilerParams(
            collective_id=0, has_side_effects=True, vmem_limit_bytes=(53 * 1024 + 256) * 1024
        ),
        cost_estimate=pl.CostEstimate(flops=400000000, bytes_accessed=3000000, transcendentals=200000),
    )(phonon, momentum, source, guess, bonds, jnp.asarray(consts))
    return pl.pallas_call(
        finish,
        out_shape=[jax.ShapeDtypeStruct(phonon.shape, f32)] * 2,
        in_specs=[vmem] * 2,
        out_specs=[hbm] * 2,
        scratch_shapes=[pltpu.SemaphoreType.DMA((2, 2))],
        compiler_params=pltpu.CompilerParams(vmem_limit_bytes=8 * 1024 * 1024),
        cost_estimate=pl.CostEstimate(flops=0, bytes_accessed=1048576, transcendentals=0),
    )(*made)


def solution(mesh):
    spec = P("tm", "band")
    return jax.shard_map(
        functools.partial(shards, mesh.shape["tm"]),
        mesh=mesh,
        in_specs=(spec, spec, spec, spec, P(None, "band", None)),
        out_specs=(spec, spec),
        check_vma=False,
    )
```
